512 devices in a mesh: region: 8 (over y), super: 64 (over x, z, core).
Axes of the slice: x: 4, y: 8, z: 8, core: 2. Of those that a mesh axis runs over, the one named last changes fastest.
Arguments:
- obs_coords: float32 [2, 2097152], P(None, ('region', 'super')), may hold values from 0 to 1, as said below
- obs_values: bfloat16 [64, 2097152], P(None, ('region', 'super')), may hold values from -6 to 6
- obs_precision: float32 [2097152], P(('region', 'super')), may hold values from 0.0009765625 to 0.009765625
- site_coords: float32 [2, 262144], P(None, ('region', 'super')), may hold values from 0 to 1, as said below
- length_scale: float32 [3], replicated, may hold values from 0.0005859375 to 0.3, as said below
- global_knots: float32 [2, 256], replicated, may hold values from 0 to 1
- region_knots: float32 [64, 2, 256], P('super'), may hold values from 0 to 1, as said below
- leaf_knots: float32 [512, 2, 256], P(('region', 'super')), may hold values from 0 to 1, as said below
- global_prior: float32 [256, 256], replicated, as said below
- region_prior: float32 [64, 256, 256], P('super'), as said below
- leaf_prior: float32 [512, 256, 256], P(('region', 'super')), as said below
Outputs:
- prediction: float32 [64, 262144], P(None, ('region', 'super'))
The draws below stay inside these ranges and needn't reach their ends.
Inputs may be any that keep to these rules, and one draw needn't show every extreme that they name: `global_prior`: symmetric; each diagonal entry exceeds the sum of magnitudes of the other entries of its row. `region_prior`: each region's matrix symmetric; each diagonal entry exceeds the sum of magnitudes of the other entries of its row. `leaf_prior`: each leaf's matrix symmetric; each diagonal entry exceeds the sum of magnitudes of the other entries of its row. `obs_coords`: the region cells tile the unit square as a grid, each split into a grid of leaf cells; leaf l's observations lie inside leaf l's cell. `site_coords`: leaf l's sites lie inside leaf l's cell. `region_knots`: region g's knots lie inside region g's cell. `leaf_knots`: leaf l's knots lie inside leaf l's cell. `length_scale`: the global scale lies in 0.15 to 0.3, the regional scale in 0.7 to 1.0 times 1 / sqrt(16384), the leaf scale in 0.3 to 0.9 times 1 / sqrt(512).
All inputs are finite; a program needn't handle non-finite values.
Results may differ from the reference program's by a relative error of at most 0.0003.
The reference program's roundings to bfloat16 on the way count: a program that leaves them out, or rounds other values in their place, can miss the bound.
Values sent between devices are 32-bit elements; how exact they have to be, the bound alone decides.
A program may use at most 64 MiB of HBM per device.

```python
import math
import jax
import jax.numpy as jnp
from jax import lax

R = 256
FIELDS = 64
NOBS = 4096
NSITE = 512
OBS = 2097152
N_REGION = 8
N_SUPER = 64


def prior_block(key, count):
    noise = jax.random.normal(key, (count, R, R), jnp.float32) * (0.08 / math.sqrt(R))
    sym = 0.5 * (noise + jnp.swapaxes(noise, 1, 2))
    eye = jnp.eye(R, dtype=jnp.float32)
    offdiag = sym * (1.0 - eye)
    diagonal = 1.25 * jnp.sum(jnp.abs(offdiag), axis=2) + 0.25
    result = offdiag + eye[None, :, :] * diagonal[:, :, None]
    return result


def draw_global_prior(key, part):
    return prior_block(jax.random.fold_in(key, 11), 1)[0]


def draw_region_prior(key, part):
    return prior_block(jax.random.fold_in(key, 12), N_SUPER)


def draw_leaf_prior(key, part):
    return prior_block(jax.random.fold_in(key, 13), N_REGION * N_SUPER)


def grid_shape(count):
    across = 1
    for divisor in range(1, count + 1):
        if count % divisor == 0 and divisor * divisor <= count:
            across = divisor
    return (count // across, across)


def region_cell(region):
    cols_r, rows_r = grid_shape(N_SUPER)
    width = 1.0 / cols_r
    height = 1.0 / rows_r
    left = (region % cols_r).astype(jnp.float32) * width
    bottom = (region // cols_r).astype(jnp.float32) * height
    return (left, bottom, width, height)


def leaf_cell(leaf):
    region = leaf % N_SUPER
    member = leaf // N_SUPER
    left, bottom, width, height = region_cell(region)
    cols_l, rows_l = grid_shape(N_REGION)
    width_l = width / cols_l
    height_l = height / rows_l
    left_l = left + (member % cols_l).astype(jnp.float32) * width_l
    bottom_l = bottom + (member // cols_l).astype(jnp.float32) * height_l
    return (left_l, bottom_l, width_l, height_l)


def place_points(key, leaf):
    left, bottom, width, height = leaf_cell(leaf)
    unit = jax.random.uniform(key, (2,) + leaf.shape, jnp.float32, 0.0, 1.0)
    return jnp.stack([left + unit[0] * width, bottom + unit[1] * height], axis=0)


def draw_obs_coords(key, part):
    leaf = jnp.arange(NOBS * N_REGION * N_SUPER, dtype=jnp.int32) // NOBS
    return place_points(jax.random.fold_in(key, 21), leaf)


def draw_site_coords(key, part):
    leaf = jnp.arange(NSITE * N_REGION * N_SUPER, dtype=jnp.int32) // NSITE
    return place_points(jax.random.fold_in(key, 22), leaf)


def draw_leaf_knots(key, part):
    leaf = jnp.broadcast_to(jnp.arange(N_REGION * N_SUPER, dtype=jnp.int32)[:, None], (N_REGION * N_SUPER, R))
    points = place_points(jax.random.fold_in(key, 23), leaf)
    return jnp.transpose(points, (1, 0, 2))


def draw_region_knots(key, part):
    region = jnp.broadcast_to(jnp.arange(N_SUPER, dtype=jnp.int32)[:, None], (N_SUPER, R))
    left, bottom, width, height = region_cell(region)
    unit = jax.random.uniform(jax.random.fold_in(key, 24), (2, N_SUPER, R), jnp.float32, 0.0, 1.0)
    points = jnp.stack([left + unit[0] * width, bottom + unit[1] * height], axis=0)
    return jnp.transpose(points, (1, 0, 2))


def draw_length_scale(key, part):
    unit = jax.random.uniform(jax.random.fold_in(key, 25), (3,), jnp.float32, 0.0, 1.0)
    spacing = 1.0 / math.sqrt(N_SUPER * R)
    lows = jnp.array([0.15, 0.7 * spacing, 0.3 / math.sqrt(N_REGION * N_SUPER)], jnp.float32)
    highs = jnp.array([0.3, spacing, 0.9 / math.sqrt(N_REGION * N_SUPER)], jnp.float32)
    return jnp.exp(jnp.log(lows) + unit * (jnp.log(highs) - jnp.log(lows)))


def level_of(rng, dims, cuts, least, high):
    def one(axis_at, blocks):
        heights = jax.random.uniform(jax.random.fold_in(jax.random.fold_in(rng, 6), axis_at), (blocks,), jnp.float32, least / len(cuts), high / len(cuts))
        return jnp.repeat(jnp.exp(heights), dims[axis_at] // blocks).reshape((-1,) + (1,) * (len(dims) - axis_at - 1))

    level = one(*cuts[0])
    for cut in cuts[1:]:
        level = level * one(*cut)
    return level


def gaussian(key, shape, deviation, reach, split=(), held_as=jnp.bfloat16):
    factor_of = level_of(key, shape, split, -0.22, 0.18) if split else 1.0
    drawn = jax.random.normal(key, shape, jnp.float32) * deviation * factor_of
    return jnp.minimum(jnp.maximum(drawn, -reach), reach).astype(held_as)


def setup_inputs(seed: int = 0) -> dict:
    splits = jax.random.split(jax.random.key(seed), 12)
    obs_coords = draw_obs_coords(jax.random.fold_in(splits[11], 71), 0)
    obs_values = gaussian(splits[1], (FIELDS, OBS), 1.0, 6.0, ((1, 512),))
    obs_precision = jnp.clip(jnp.exp(math.log(0.009765625) - 2.3025851 * jax.random.uniform(splits[2], (OBS,), jnp.float32) ** level_of(splits[2], (OBS,), ((0, 512),), -0.2, 0.2)), 0.0009765625, 0.009765625)
    site_coords = draw_site_coords(jax.random.fold_in(splits[11], 71), 0)
    length_scale = draw_length_scale(jax.random.fold_in(splits[11], 71), 0)
    global_knots = jnp.clip(jax.random.uniform(splits[5], (2, R), jnp.float32, 0.0, 1.0), 0.0, 1.0)
    region_knots = draw_region_knots(jax.random.fold_in(splits[11], 71), 0)
    leaf_knots = draw_leaf_knots(jax.random.fold_in(splits[11], 71), 0)
    global_prior = draw_global_prior(jax.random.fold_in(splits[11], 71), 0)
    region_prior = draw_region_prior(jax.random.fold_in(splits[11], 71), 0)
    leaf_prior = draw_leaf_prior(jax.random.fold_in(splits[11], 71), 0)
    return dict(obs_coords=obs_coords, obs_values=obs_values, obs_precision=obs_precision, site_coords=site_coords, length_scale=length_scale, global_knots=global_knots, region_knots=region_knots, leaf_knots=leaf_knots, global_prior=global_prior, region_prior=region_prior, leaf_prior=leaf_prior)


HIGH = lax.Precision.HIGHEST

def basis_rows(coords, knots, scale):
    diff_x = coords[0][:, None] - knots[0][None, :]
    diff_y = coords[1][:, None] - knots[1][None, :]
    return jnp.exp(-0.5 * (diff_x * diff_x + diff_y * diff_y) / (scale * scale))

def basis_cols(knots, coords, scale):
    diff_x = knots[0][:, None] - coords[0][None, :]
    diff_y = knots[1][:, None] - coords[1][None, :]
    return jnp.exp(-0.5 * (diff_x * diff_x + diff_y * diff_y) / (scale * scale))

def leaf_terms(coords, values, precision, knots_g, knots_r, knots_l, scales, prior_l):
    weight = jnp.sqrt(precision)[:, None]
    stacked = jnp.concatenate([basis_rows(coords, knots_g, scales[0]), basis_rows(coords, knots_r, scales[1]), basis_rows(coords, knots_l, scales[2]), values.astype(jnp.float32).T], axis=1)
    scaled = (stacked * weight).astype(jnp.bfloat16).astype(jnp.float32)
    gram = jnp.dot(scaled.T, scaled, precision=HIGH)
    cross = gram[2 * R:3 * R, :2 * R]
    factor = jnp.linalg.cholesky(prior_l + gram[2 * R:3 * R, 2 * R:3 * R])
    rhs = jnp.concatenate([cross, gram[2 * R:3 * R, 3 * R:]], axis=1)
    solved = jax.scipy.linalg.cho_solve((factor, True), rhs)
    left = jnp.concatenate([gram[:2 * R, :2 * R], gram[:2 * R, 3 * R:]], axis=1)
    schur = left - jnp.dot(cross.T, solved, precision=HIGH)
    return (schur, solved)

def region_terms(rows, prior_r):
    factor = jnp.linalg.cholesky(prior_r + rows[:, R:2 * R])
    rhs = jnp.concatenate([rows[:, :R], rows[:, 2 * R:]], axis=1)
    solved = jax.scipy.linalg.cho_solve((factor, True), rhs)
    correction = jnp.dot(rows[:, :R].T, solved, precision=HIGH)
    return (solved, correction)

def global_part(schur):
    return jnp.concatenate([schur[:R, :R], schur[:R, 2 * R:]], axis=1)

def reference(obs_coords, obs_values, obs_precision, site_coords, length_scale, global_knots, region_knots, leaf_knots, global_prior, region_prior, leaf_prior):
    coords = obs_coords.reshape(2, N_REGION, N_SUPER, NOBS)
    values = obs_values.reshape(FIELDS, N_REGION, N_SUPER, NOBS)
    precision = obs_precision.reshape(N_REGION, N_SUPER, NOBS)
    sites = site_coords.reshape(2, N_REGION, N_SUPER, NSITE)
    knots_leaf = leaf_knots.reshape(N_REGION, N_SUPER, 2, R)
    prior_leaf = leaf_prior.reshape(N_REGION, N_SUPER, R, R)

    def one_region(index):

        def step(total, member):
            schur, solved = leaf_terms(coords[:, member, index], values[:, member, index], precision[member, index], global_knots, region_knots[index], knots_leaf[member, index], length_scale, prior_leaf[member, index])
            return (total + schur, solved)
        start = jnp.zeros((2 * R, 2 * R + FIELDS), jnp.float32)
        total, solved = lax.scan(step, start, jnp.arange(N_REGION))
        region_solved, correction = region_terms(total[R:2 * R], region_prior[index])
        return (global_part(total) - correction, region_solved, solved)
    pieces, region_solved, leaf_solved = lax.map(one_region, jnp.arange(N_SUPER))
    upper = lax.optimization_barrier(jnp.sum(pieces, axis=0))
    factor = jnp.linalg.cholesky(global_prior + upper[:, :R])
    global_weights = jax.scipy.linalg.cho_solve((factor, True), upper[:, R:])

    def predict_region(index):
        solved_r = region_solved[index]
        region_weights = solved_r[:, R:] - jnp.dot(solved_r[:, :R], global_weights, precision=HIGH)
        upper_weights = jnp.concatenate([global_weights, region_weights], axis=0)

        def predict_leaf(member):
            solved_l = leaf_solved[index, member]
            leaf_weights = solved_l[:, 2 * R:] - jnp.dot(solved_l[:, :2 * R], upper_weights, precision=HIGH)
            weights = jnp.concatenate([upper_weights, leaf_weights], axis=0)
            place = sites[:, member, index]
            table = jnp.concatenate([basis_cols(global_knots, place, length_scale[0]), basis_cols(region_knots[index], place, length_scale[1]), basis_cols(knots_leaf[member, index], place, length_scale[2])], axis=0)
            return jnp.dot(weights.T, table, precision=HIGH)
        return lax.map(predict_leaf, jnp.arange(N_REGION))
    blocks = lax.map(predict_region, jnp.arange(N_SUPER))
    return jnp.transpose(blocks, (2, 1, 0, 3)).reshape(FIELDS, N_REGION * N_SUPER * NSITE)
```

```python
import functools

import jax
import jax.numpy as jnp
from jax import lax
from jax.experimental import pallas as pl
from jax.experimental.pallas import tpu as pltpu
from jax.sharding import Mesh
from jax.sharding import PartitionSpec as P

R = 256
B = 8
H = 128
FIELDS = 64
F32 = jnp.float32
BF16 = jnp.bfloat16
HIGH = lax.Precision.HIGHEST
MESH = pl.DeviceIdType.MESH
REGION_SUPER = ("region", "super_0", "super_1", "super_2")
SUPER = ("super_0", "super_1", "super_2")
VMEM = pl.BlockSpec(memory_space=pltpu.VMEM)
SMEM = pl.BlockSpec(memory_space=pltpu.SMEM)
LIMIT = 40 * 1024 * 1024


def parts_of(x):
    high = x.astype(BF16).astype(F32)
    rest = x - high
    middle = rest.astype(BF16).astype(F32)
    return high, middle, rest - middle


def left_stack(x):
    h, m, l = parts_of(x)
    return jnp.concatenate([h, h, m, h, l, m], axis=0).astype(BF16)


def right_stack(x):
    h, m, l = parts_of(x)
    return jnp.concatenate([h, m, h, l, h, m], axis=0).astype(BF16)


def total_of(terms):
    terms = list(terms)
    while len(terms) > 1:
        pairs = [terms[i] + terms[i + 1] for i in range(0, len(terms) - 1, 2)]
        terms = pairs + terms[len(pairs) * 2 :]
    return terms[0]


def columns_of(x, first):
    zero = jnp.zeros((B, H), jnp.int32)
    return [jnp.take_along_axis(x, zero + (first + j), axis=1) for j in range(B)]


def row_of(ref, r):
    return jnp.broadcast_to(ref[r : r + 1, :], (B, ref.shape[1]))


def twice(x):
    return jnp.concatenate([x, x], axis=1)


def eliminate(f_ref, w_ref, v_ref, cols_ref, rows_ref, lh_ref, xh_ref, between=None):
    lane = lax.broadcasted_iota(jnp.int32, (B, R), 1)
    sub = lax.broadcasted_iota(jnp.int32, (B, R), 0)
    sub_half = lax.broadcasted_iota(jnp.int32, (B, H), 0)
    lane_all = lax.broadcasted_iota(jnp.int32, (R, R), 1)
    lh_ref[...] = jnp.zeros_like(lh_ref)
    xh_ref[...] = jnp.zeros_like(xh_ref)

    def body(k, panel):
        base = pl.multiple_of(k * B, B)
        half = lax.div(k, 16)
        at = (k - 16 * half) * B
        diag = jnp.where(half == 0, panel[:, :H], panel[:, H:])
        for j, column in enumerate(columns_of(diag, at)):
            cols_ref[j * B : (j + 1) * B, :] = column
        mark = (lane >= base) & (lane < base + B)
        eye = jnp.where(lane == base + sub, 1.0, 0.0).astype(F32)
        rows_ref[...] = jnp.where(mark, eye, panel)
        update = lax.dot_general(
            lh_ref[...], xh_ref[...], (((0,), (0,)), ((), ())), preferred_element_type=F32
        )
        last = (lane_all >= base - B) & (lane_all < base)
        f_ref[...] = jnp.where(last, 0.0, f_ref[...]) - update
        s = {}
        for j in range(B):
            for i in range(j + 1):
                s[i, j] = row_of(cols_ref, j * B + i)
        low = {}
        inv = []
        for p in range(B):
            inv.append(1.0 / s[p, p])
            for i in range(p + 1, B):
                m = s[p, i] * inv[p]
                for j in range(i, B):
                    s[i, j] = s[i, j] - m * s[p, j]
                for c in range(p):
                    low[i, c] = low[i, c] - m * low[p, c]
                low[i, p] = -m
        following = pl.multiple_of(jnp.minimum(k + 1, R // B - 1) * B, B)
        ahead = f_ref[pl.ds(following, B), :]
        g = columns_of(jnp.where(half == 0, ahead[:, :H], ahead[:, H:]), at)
        rows = [row_of(rows_ref, j) for j in range(B)]
        row = [total_of([twice(low[j, m]) * rows[m] for m in range(j)] + [rows[j]]) for j in range(B)]
        lcol = [total_of([g[m] * low[j, m] for m in range(j)] + [g[j]]) * inv[j] for j in range(B)]
        panel_next = jnp.where(mark, 0.0, ahead) - total_of(
            [twice(lcol[j]) * row[j] for j in range(B)]
        )
        dcol = inv[0]
        mine = row[0]
        for i in range(1, B):
            dcol = jnp.where(sub_half == i, inv[i], dcol)
            mine = jnp.where(sub == i, row[i], mine)
        x = twice(dcol) * mine
        done = lane < base + B
        w_ref[pl.ds(base, B), :] = jnp.where(done, mine, 0.0)
        v_ref[pl.ds(base, B), :] = jnp.where(done, x, 0.0)
        lh_ref[...] = left_stack(jnp.where(done, 0.0, mine))
        xh_ref[...] = right_stack(x)
        return panel_next

    if between is None:
        lax.fori_loop(0, R // B, body, f_ref[0:B, :])
    else:
        panel = lax.fori_loop(0, R // B // 2, body, f_ref[0:B, :])
        between()
        lax.fori_loop(R // B // 2, R // B, body, panel)


def eliminate_scratch():
    return [
        pltpu.VMEM((R, R), F32),
        pltpu.VMEM((B * B, H), F32),
        pltpu.VMEM((B, R), F32),
        pltpu.VMEM((48, R), BF16),
        pltpu.VMEM((48, R), BF16),
    ]


def dot(a, b):
    return jnp.dot(a, b, precision=HIGH, preferred_element_type=F32)


def dot_t(a, b):
    return lax.dot_general(a, b, (((0,), (0,)), ((), ())), precision=HIGH, preferred_element_type=F32)


def gram_of(a, b):
    return lax.dot_general(a, b, (((1,), (1,)), ((), ())), preferred_element_type=F32)


def upright(knots):
    spare = jnp.zeros((6, R), F32)
    return jnp.concatenate([knots, spare], axis=0).T


def basis(knots, places, scale):
    diff_x = knots[:, 0:1] - places[0:1, :]
    diff_y = knots[:, 1:2] - places[1:2, :]
    return jnp.exp((diff_x * diff_x + diff_y * diff_y) * scale)


def factors(scale_ref):
    return [-0.5 / (scale_ref[i] * scale_ref[i]) for i in range(3)]


CHUNK = 512


def leaf_kernel(
    scale_ref, gk_hbm, rk_hbm, lk_hbm, coords_hbm, precision_hbm, values_hbm, sites_hbm, prior_hbm,
    mc_ref, gs_ref, t2_ref, w_ref, table_ref,
    gk_ref, rk_ref, lk_ref, coords_ref, precision_ref, values_ref, sites_ref, prior_ref, sems,
    z_ref, gv_ref, gr_ref, gg_ref, v_ref, f_ref, *scratch,
):
    sources = (gk_hbm, rk_hbm, lk_hbm, coords_hbm, precision_hbm, values_hbm, sites_hbm, prior_hbm)
    targets = (gk_ref, rk_ref, lk_ref, coords_ref, precision_ref, values_ref, sites_ref, prior_ref)
    copies = [pltpu.make_async_copy(a, b, sems.at[n]) for n, (a, b) in enumerate(zip(sources, targets))]
    for copy in copies:
        copy.start()
    for copy in copies[:6]:
        copy.wait()
    scale = factors(scale_ref)
    knots = [upright(lk_ref[...]), upright(rk_ref[...]), upright(gk_ref[...])]
    scales = [scale[2], scale[1], scale[0]]
    gv_ref[...] = jnp.zeros_like(gv_ref)
    gr_ref[...] = jnp.zeros_like(gr_ref)
    gg_ref[...] = jnp.zeros_like(gg_ref)

    def step(i, _):
        at = pl.ds(pl.multiple_of(i * CHUNK, CHUNK), CHUNK)
        places = coords_ref[:, at]
        weight = jnp.sqrt(precision_ref[:, at])
        for n in range(3):
            z_ref[n * R : (n + 1) * R, :] = (basis(knots[n], places, scales[n]) * weight).astype(BF16)
        z_ref[3 * R :, :] = (values_ref[:, at].astype(F32) * weight).astype(BF16)
        gv_ref[...] += gram_of(z_ref[:R, :], z_ref[...])
        gr_ref[...] += gram_of(z_ref[R : 2 * R, :], z_ref[R:, :])
        gg_ref[...] += gram_of(z_ref[2 * R : 3 * R, :], z_ref[2 * R :, :])
        return 0

    lax.fori_loop(0, coords_ref.shape[1] // CHUNK, step, 0)
    for copy in copies[6:]:
        copy.wait()
    for n, (k, s) in enumerate(zip(knots[::-1], scales[::-1])):
        order = n
        table_ref[order * R : (order + 1) * R, :] = basis(k, sites_ref[...], s)
    f_ref[...] = prior_ref[...] + gv_ref[:, :R]
    eliminate(f_ref, w_ref, v_ref, *scratch)
    t1 = dot(w_ref[...], gv_ref[:, R:])
    t2 = dot(v_ref[...], gv_ref[:, R:])
    t2_ref[...] = t2
    regional = gr_ref[...] - dot_t(t1[:, :R], t2)
    upper = gg_ref[...] - dot_t(t1[:, R : 2 * R], t2[:, R:])
    mc_ref[0:H, :] = regional[:H, :H]
    mc_ref[H : 2 * H, :] = regional[H:, :H]
    mc_ref[2 * H : 3 * H, :] = regional[H:, H:R]
    for r in range(2):
        for c in range(2):
            n = 3 + 2 * r + c
            mc_ref[n * H : (n + 1) * H, :] = regional[r * H : (r + 1) * H, R + c * H : R + (c + 1) * H]
    mc_ref[7 * H :, :] = jnp.concatenate([regional[:H, 2 * R :], regional[H:, 2 * R :]], axis=1)
    pack_global(gs_ref, upper)


def pack_global(out_ref, upper):
    out_ref[0:H, :] = upper[:H, :H]
    out_ref[H : 2 * H, :] = upper[H:, :H]
    out_ref[2 * H : 3 * H, :] = upper[H:, H:R]
    out_ref[3 * H :, :] = jnp.concatenate([upper[:H, R:], upper[H:, R:]], axis=1)


def whole_of(ref, first):
    a, b, c = (ref[(first + n) * H : (first + n + 1) * H, :] for n in range(3))
    return jnp.concatenate(
        [jnp.concatenate([a, b.T], axis=1), jnp.concatenate([b, c], axis=1)], axis=0
    )


def fields_of(ref, block):
    y = ref[block * H : (block + 1) * H, :]
    return jnp.concatenate([y[:, :FIELDS], y[:, FIELDS:]], axis=0)


def shape(*dims):
    return jax.ShapeDtypeStruct(dims, F32)


def leaf(scales, coords, values, precision, gk, rk, lk, prior, sites):
    operands = (gk, rk, lk, coords, precision, values, sites, prior)
    return pl.pallas_call(
        leaf_kernel,
        name="leaf",
        out_shape=[
            shape(8 * H, H), shape(4 * H, H), shape(R, 2 * R + FIELDS), shape(R, R),
            shape(3 * R, sites.shape[1]),
        ],
        in_specs=[SMEM] + [pl.BlockSpec(memory_space=pl.ANY)] * 8,
        out_specs=[VMEM] * 5,
        scratch_shapes=[pltpu.VMEM(a.shape, a.dtype) for a in operands]
        + [pltpu.SemaphoreType.DMA((8,))]
        + [
            pltpu.VMEM((3 * R + FIELDS, CHUNK), BF16),
            pltpu.VMEM((R, 3 * R + FIELDS), F32),
            pltpu.VMEM((R, 2 * R + FIELDS), F32),
            pltpu.VMEM((R, R + FIELDS), F32),
            pltpu.VMEM((R, R), F32),
        ] + eliminate_scratch(),
        compiler_params=pltpu.CompilerParams(vmem_limit_bytes=LIMIT),
    )(scales, *operands)


NY, NX, NZ, NC = 8, 4, 8, 2
GROUP = [(dx, dc) for dx in range(NX) for dc in range(NC)][1:]


def here():
    return (
        lax.axis_index("region"),
        lax.axis_index("super_0"),
        lax.axis_index("super_1"),
        lax.axis_index("super_2"),
    )


def on_y(d):
    y, x, z, c = here()
    return (lax.rem(y + d, NY), x, z, c)


def on_z(d):
    y, x, z, c = here()
    return (y, x, lax.rem(z + d, NZ), c)


def on_xc(d):
    y, x, z, c = here()
    return (y, lax.rem(x + d[0], NX), z, lax.rem(c + d[1], NC))


def greet(places):
    barrier = pltpu.get_barrier_semaphore()
    for place in places:
        pl.semaphore_signal(barrier, inc=1, device_id=place, device_id_type=MESH)
    pl.semaphore_wait(barrier, len(places))


def send(source, target, sems, n, place):
    copy = pltpu.make_async_remote_copy(
        src_ref=source,
        dst_ref=target,
        send_sem=sems[0].at[n],
        recv_sem=sems[1].at[n],
        device_id=place,
        device_id_type=MESH,
    )
    copy.start()
    return copy


def arrived(copies):
    for copy in copies:
        copy.wait_recv()


def sent(copies):
    for copy in copies:
        copy.wait_send()


def added(own, arrivals_ref):
    return total_of([own] + [arrivals_ref[n] for n in range(arrivals_ref.shape[0])])


def pair_of_sems(count):
    return [pltpu.SemaphoreType.DMA((count,)), pltpu.SemaphoreType.DMA((count,))]


M_ROWS, C_ROWS = 3 * H, 5 * H
M_PART, C_PART = M_ROWS // NY, C_ROWS // NY


def region_kernel(
    mc_ref, gs_ref, prior_hbm,
    corr_ref, share_ref, t2_ref, w_ref,
    m_ref, c_ref, m_in, c_in, g_in, g_sum, y_in, prior_ref, v_ref,
    prior_sem, s0, r0, s1, r1, s2, r2, s3, r3, s4, r4, s5, r5,
    f_ref, *scratch,
):
    y, x, z, c = here()
    prior_copy = pltpu.make_async_copy(prior_hbm, prior_ref, prior_sem)
    prior_copy.start()
    greet([on_y(d) for d in range(1, NY)] + [on_xc(d) for d in GROUP])
    started = []

    def scatter(rows, first, part, target, sems):
        copies = []
        for d in range(1, NY):
            place = on_y(d)
            at = pl.ds(pl.multiple_of(first + place[0] * part, 8), part)
            copies.append(send(rows.at[at, :], target.at[d - 1], sems, d - 1, place))
        started.extend(copies)
        return copies

    def gather(ref, part, sems):
        at = pl.ds(pl.multiple_of(y * part, 8), part)
        copies = [send(ref.at[at, :], ref.at[at, :], sems, d - 1, on_y(d)) for d in range(1, NY)]
        started.extend(copies)
        return copies

    m_scatter = scatter(mc_ref, 0, M_PART, m_in, (s0, r0))
    g_scatter = []
    for n, d in enumerate(GROUP):
        place = on_xc(d)
        g_scatter.append(send(gs_ref.at[place[3], :, place[1]], g_in.at[n], (s1, r1), n, place))
    started.extend(g_scatter)
    arrived(m_scatter)
    own = pl.ds(pl.multiple_of(y * M_PART, 8), M_PART)
    m_ref[own, :] = added(mc_ref[own, :], m_in)
    m_gather = gather(m_ref, M_PART, (s2, r2))
    c_scatter = scatter(mc_ref, M_ROWS, C_PART, c_in, (s3, r3))
    arrived(m_gather)
    prior_copy.wait()
    f_ref[...] = prior_ref[...] + whole_of(m_ref, 0)
    later = {}

    def between():
        arrived(c_scatter)
        mine = pl.ds(pl.multiple_of(y * C_PART, 8), C_PART)
        theirs = pl.ds(pl.multiple_of(M_ROWS + y * C_PART, 8), C_PART)
        c_ref[mine, :] = added(mc_ref[theirs, :], c_in)
        later["c"] = gather(c_ref, C_PART, (s4, r4))
        arrived(g_scatter)
        g_sum[...] = added(gs_ref[c, :, x], g_in)
        later["y"] = []
        for d in range(1, NY):
            place = on_y(d)
            later["y"].append(send(g_sum.at[place[0]], y_in.at[d - 1], (s5, r5), d - 1, place))
        started.extend(later["y"])

    eliminate(f_ref, w_ref, v_ref, *scratch, between=between)
    arrived(later["c"])
    arrived(later["y"])
    share_ref[...] = added(g_sum[y], y_in)
    cross = jnp.concatenate(
        [
            jnp.concatenate([c_ref[(2 * r + n) * H : (2 * r + n + 1) * H, :] for n in range(2)], axis=1)
            for r in range(2)
        ],
        axis=0,
    )
    rhs = jnp.concatenate([cross, fields_of(c_ref, 4)], axis=1)
    t1 = dot(w_ref[...], cross)
    t2 = dot(v_ref[...], rhs)
    t2_ref[...] = t2
    pack_global(corr_ref, dot_t(t1, t2))
    sent(started)


def region(mc, gs, prior):
    sems = []
    for _ in range(6):
        sems += pair_of_sems(7)
    return pl.pallas_call(
        region_kernel,
        name="region",
        out_shape=[shape(4 * H, H), shape(B, H), shape(R, R + FIELDS), shape(R, R)],
        in_specs=[VMEM, VMEM, pl.BlockSpec(memory_space=pl.ANY)],
        out_specs=[VMEM] * 4,
        scratch_shapes=[
            pltpu.VMEM((M_ROWS, H), F32),
            pltpu.VMEM((C_ROWS, H), F32),
            pltpu.VMEM((NY - 1, M_PART, H), F32),
            pltpu.VMEM((NY - 1, C_PART, H), F32),
            pltpu.VMEM((7, NY, B, H), F32),
            pltpu.VMEM((NY, B, H), F32),
            pltpu.VMEM((NY - 1, B, H), F32),
            pltpu.VMEM((R, R), F32),
            pltpu.VMEM((R, R), F32),
            pltpu.SemaphoreType.DMA,
        ] + sems + [pltpu.VMEM((R, R), F32)] + eliminate_scratch()[1:],
        compiler_params=pltpu.CompilerParams(
            vmem_limit_bytes=LIMIT, collective_id=0, has_side_effects=True
        ),
    )(mc, gs, prior)


def upper_kernel(corr_ref, share_ref, out_ref, k_in, z_in, s0, r0, s1, r1, s2, r2, s3, r3, s4, r4):
    y, x, z, c = here()
    greet(
        [on_xc(d) for d in GROUP]
        + [on_z(d) for d in range(1, NZ)]
        + [on_y(d) for d in range(1, NY)]
    )
    started = []
    first = []
    for n, d in enumerate(GROUP):
        place = on_xc(d)
        first.append(send(corr_ref.at[place[3], y, place[1]], k_in.at[n], (s0, r0), n, place))
    arrived(first)
    z_in[z] = share_ref[...] - added(corr_ref[c, y, x], k_in)
    second = [send(z_in.at[z], z_in.at[z], (s1, r1), d - 1, on_z(d)) for d in range(1, NZ)]
    arrived(second)
    out_ref[c, y, x] = total_of([z_in[n] for n in range(NZ)])
    third = [
        send(out_ref.at[c, y, x], out_ref.at[c, y, x], (s2, r2), dx - 1, on_xc((dx, 0)))
        for dx in range(1, NX)
    ]
    arrived(third)
    fourth = [send(out_ref.at[c, y], out_ref.at[c, y], (s3, r3), d - 1, on_y(d)) for d in range(1, NY)]
    fifth = [send(out_ref.at[c, y], out_ref.at[c, y], (s4, r4), 0, on_xc((0, 1)))]
    for d in range(1, NY):
        fourth[d - 1].wait_recv()
        block = out_ref.at[c, lax.rem(y - d + NY, NY)]
        fifth.append(send(block, block, (s4, r4), d, on_xc((0, 1))))
    arrived(fifth)
    sent(first + second + third + fourth + fifth)


def upper_of(corr, share):
    sems = []
    for count in (7, 7, 3, 7, 8):
        sems += pair_of_sems(count)
    return pl.pallas_call(
        upper_kernel,
        name="upper",
        out_shape=shape(NC, NY, NX, B, H),
        in_specs=[VMEM] * 2,
        out_specs=VMEM,
        scratch_shapes=[pltpu.VMEM((7, B, H), F32), pltpu.VMEM((NZ, B, H), F32)] + sems,
        compiler_params=pltpu.CompilerParams(collective_id=1, has_side_effects=True),
    )(corr, share)


def tail_kernel(up_ref, prior_ref, w_r_ref, t2_r_ref, w_l_ref, t2_l_ref, table_ref, out_ref, w_ref, v_ref, f_ref, *scratch):
    f_ref[...] = prior_ref[...] + whole_of(up_ref, 0)
    eliminate(f_ref, w_ref, v_ref, *scratch)
    g = dot_t(w_ref[...], dot(v_ref[...], fields_of(up_ref, 3)))
    r = dot_t(w_r_ref[...], t2_r_ref[:, R:] - dot(t2_r_ref[:, :R], g))
    rest = t2_l_ref[:, 2 * R :] - dot(t2_l_ref[:, : 2 * R], jnp.concatenate([r, g], axis=0))
    l = dot_t(w_l_ref[...], rest)
    out_ref[...] = dot_t(jnp.concatenate([g, r, l], axis=0), table_ref[...])


def tail(up, prior, w_r, t2_r, w_l, t2_l, table):
    return pl.pallas_call(
        tail_kernel,
        name="tail",
        out_shape=shape(FIELDS, table.shape[1]),
        in_specs=[VMEM] * 7,
        out_specs=VMEM,
        scratch_shapes=[pltpu.VMEM((R, R), F32)] * 2 + eliminate_scratch(),
        compiler_params=pltpu.CompilerParams(vmem_limit_bytes=LIMIT),
    )(up, prior, w_r, t2_r, w_l, t2_l, table)


def shards(
    obs_coords,
    obs_values,
    obs_precision,
    site_coords,
    length_scale,
    global_knots,
    region_knots,
    leaf_knots,
    global_prior,
    region_prior,
    leaf_prior,
):
    mc, gs, t2, w, table = leaf(
        length_scale,
        obs_coords,
        obs_values,
        obs_precision[None],
        global_knots,
        region_knots[0],
        leaf_knots[0],
        leaf_prior[0],
        site_coords,
    )
    tiles = (NC, NY, NX, B, H)
    corr, share, t2_r, w_r = region(mc, gs.reshape(tiles), region_prior[0])
    upper = upper_of(corr.reshape(tiles), share)
    return tail(upper.reshape(4 * H, H), global_prior, w_r, t2_r, w, t2, table)


def solution(mesh):
    split = Mesh(
        mesh.devices.reshape(NY, NX, NZ, NC),
        ("region", "super_0", "super_1", "super_2"),
    )
    return jax.shard_map(
        shards,
        mesh=split,
        in_specs=(
            P(None, REGION_SUPER),
            P(None, REGION_SUPER),
            P(REGION_SUPER),
            P(None, REGION_SUPER),
            P(),
            P(),
            P(SUPER, None, None),
            P(REGION_SUPER, None, None),
            P(),
            P(SUPER, None, None),
            P(REGION_SUPER, None, None),
        ),
        out_specs=P(None, REGION_SUPER),
        check_vma=False,
    )
```

```python
import functools

import jax
import jax.numpy as jnp
from jax import lax
from jax.experimental import pallas as pl
from jax.experimental.pallas import tpu as pltpu
from jax.sharding import Mesh
from jax.sharding import PartitionSpec as P

R = 256
B = 8
H = 128
FIELDS = 64
F32 = jnp.float32
BF16 = jnp.bfloat16
HIGH = lax.Precision.HIGHEST
MESH = pl.DeviceIdType.MESH
REGION_SUPER = ("region", "super_0", "super_1", "super_2")
SUPER = ("super_0", "super_1", "super_2")
VMEM = pl.BlockSpec(memory_space=pltpu.VMEM)
SMEM = pl.BlockSpec(memory_space=pltpu.SMEM)
LIMIT = 60 * 1024 * 1024


def parts_of(x):
    high = x.astype(BF16).astype(F32)
    rest = x - high
    middle = rest.astype(BF16).astype(F32)
    return high, middle, rest - middle


def left_stack(x):
    h, m, l = parts_of(x)
    return jnp.concatenate([h, h, m, h, l, m], axis=0).astype(BF16)


def right_stack(x):
    h, m, l = parts_of(x)
    return jnp.concatenate([h, m, h, l, h, m], axis=0).astype(BF16)


def total_of(terms):
    terms = list(terms)
    while len(terms) > 1:
        pairs = [terms[i] + terms[i + 1] for i in range(0, len(terms) - 1, 2)]
        terms = pairs + terms[len(pairs) * 2 :]
    return terms[0]


def columns_of(x, first):
    zero = jnp.zeros((B, H), jnp.int32)
    return [jnp.take_along_axis(x, zero + (first + j), axis=1) for j in range(B)]


def row_of(ref, r):
    return jnp.broadcast_to(ref[r : r + 1, :], (B, ref.shape[1]))


def twice(x):
    return jnp.concatenate([x, x], axis=1)


def eliminate(f_ref, w_ref, v_ref, cols_ref, rows_ref, lh_ref, xh_ref, between=None):
    lane = lax.broadcasted_iota(jnp.int32, (B, R), 1)
    sub = lax.broadcasted_iota(jnp.int32, (B, R), 0)
    sub_half = lax.broadcasted_iota(jnp.int32, (B, H), 0)
    lane_all = lax.broadcasted_iota(jnp.int32, (R, R), 1)
    lh_ref[...] = jnp.zeros_like(lh_ref)
    xh_ref[...] = jnp.zeros_like(xh_ref)

    def body(k, panel):
        base = pl.multiple_of(k * B, B)
        half = lax.div(k, 16)
        at = (k - 16 * half) * B
        diag = jnp.where(half == 0, panel[:, :H], panel[:, H:])
        for j, column in enumerate(columns_of(diag, at)):
            cols_ref[j * B : (j + 1) * B, :] = column
        mark = (lane >= base) & (lane < base + B)
        eye = jnp.where(lane == base + sub, 1.0, 0.0).astype(F32)
        rows_ref[...] = jnp.where(mark, eye, panel)
        update = lax.dot_general(
            lh_ref[...], xh_ref[...], (((0,), (0,)), ((), ())), preferred_element_type=F32
        )
        last = (lane_all >= base - B) & (lane_all < base)
        f_ref[...] = jnp.where(last, 0.0, f_ref[...]) - update
        s = {}
        for j in range(B):
            for i in range(j + 1):
                s[i, j] = row_of(cols_ref, j * B + i)
        low = {}
        inv = []
        for p in range(B):
            inv.append(1.0 / s[p, p])
            for i in range(p + 1, B):
                m = s[p, i] * inv[p]
                for j in range(i, B):
                    s[i, j] = s[i, j] - m * s[p, j]
                for c in range(p):
                    low[i, c] = low[i, c] - m * low[p, c]
                low[i, p] = -m
        following = pl.multiple_of(jnp.minimum(k + 1, R // B - 1) * B, B)
        ahead = f_ref[pl.ds(following, B), :]
        g = columns_of(jnp.where(half == 0, ahead[:, :H], ahead[:, H:]), at)
        rows = [row_of(rows_ref, j) for j in range(B)]
        row = [total_of([twice(low[j, m]) * rows[m] for m in range(j)] + [rows[j]]) for j in range(B)]
        lcol = [total_of([g[m] * low[j, m] for m in range(j)] + [g[j]]) * inv[j] for j in range(B)]
        panel_next = jnp.where(mark, 0.0, ahead) - total_of(
            [twice(lcol[j]) * row[j] for j in range(B)]
        )
        dcol = inv[0]
        mine = row[0]
        for i in range(1, B):
            dcol = jnp.where(sub_half == i, inv[i], dcol)
            mine = jnp.where(sub == i, row[i], mine)
        x = twice(dcol) * mine
        done = lane < base + B
        w_ref[pl.ds(base, B), :] = jnp.where(done, mine, 0.0)
        v_ref[pl.ds(base, B), :] = jnp.where(done, x, 0.0)
        lh_ref[...] = left_stack(jnp.where(done, 0.0, mine))
        xh_ref[...] = right_stack(x)
        return panel_next

    if between is None:
        lax.fori_loop(0, R // B, body, f_ref[0:B, :])
    else:
        panel = lax.fori_loop(0, R // B // 2, body, f_ref[0:B, :])
        between()
        lax.fori_loop(R // B // 2, R // B, body, panel)


def eliminate_scratch():
    return [
        pltpu.VMEM((R, R), F32),
        pltpu.VMEM((B * B, H), F32),
        pltpu.VMEM((B, R), F32),
        pltpu.VMEM((48, R), BF16),
        pltpu.VMEM((48, R), BF16),
    ]


def dot(a, b):
    return jnp.dot(a, b, precision=HIGH, preferred_element_type=F32)


def dot_t(a, b):
    return lax.dot_general(a, b, (((0,), (0,)), ((), ())), precision=HIGH, preferred_element_type=F32)


def gram_of(a, b):
    return lax.dot_general(a, b, (((1,), (1,)), ((), ())), preferred_element_type=F32)


def upright(knots):
    spare = jnp.zeros((6, R), F32)
    return jnp.concatenate([knots, spare], axis=0).T


def basis(knots, places, scale):
    diff_x = knots[:, 0:1] - places[0:1, :]
    diff_y = knots[:, 1:2] - places[1:2, :]
    return jnp.exp((diff_x * diff_x + diff_y * diff_y) * scale)


def factors(scale_ref):
    return [-0.5 / (scale_ref[i] * scale_ref[i]) for i in range(3)]


CHUNK = 512


def pack_global(out_ref, upper):
    rows = [
        upper[:H, :H],
        upper[H:, :H],
        upper[H:, H:R],
        jnp.concatenate([upper[:H, R:], upper[H:, R:]], axis=1),
    ]
    out_ref[...] = jnp.concatenate(rows, axis=0).reshape(out_ref.shape)


def whole_of(ref, first):
    a, b, c = (ref[(first + n) * H : (first + n + 1) * H, :] for n in range(3))
    return jnp.concatenate(
        [jnp.concatenate([a, b.T], axis=1), jnp.concatenate([b, c], axis=1)], axis=0
    )


def fields_of(ref, block):
    y = ref[block * H : (block + 1) * H, :]
    return jnp.concatenate([y[:, :FIELDS], y[:, FIELDS:]], axis=0)


def shape(*dims):
    return jax.ShapeDtypeStruct(dims, F32)


NY, NX, NZ, NC = 8, 4, 8, 2
GROUP = [(dx, dc) for dx in range(NX) for dc in range(NC)][1:]


def here():
    return (
        lax.axis_index("region"),
        lax.axis_index("super_0"),
        lax.axis_index("super_1"),
        lax.axis_index("super_2"),
    )


def on_y(d):
    y, x, z, c = here()
    return (lax.rem(y + d, NY), x, z, c)


def on_z(d):
    y, x, z, c = here()
    return (y, x, lax.rem(z + d, NZ), c)


def on_xc(d):
    y, x, z, c = here()
    return (y, lax.rem(x + d[0], NX), z, lax.rem(c + d[1], NC))


def greet(places):
    barrier = pltpu.get_barrier_semaphore()
    for place in places:
        pl.semaphore_signal(barrier, inc=1, device_id=place, device_id_type=MESH)
    return lambda: pl.semaphore_wait(barrier, len(places))


def send(source, target, sems, n, place):
    copy = pltpu.make_async_remote_copy(
        src_ref=source,
        dst_ref=target,
        send_sem=sems[0].at[n],
        recv_sem=sems[1].at[n],
        device_id=place,
        device_id_type=MESH,
    )
    copy.start()
    return copy


def arrived(copies):
    for copy in copies:
        copy.wait_recv()


def sent(copies):
    for copy in copies:
        copy.wait_send()


def added(own, arrivals_ref):
    return total_of([own] + [arrivals_ref[n] for n in range(arrivals_ref.shape[0])])


def pair_of_sems(count):
    return [pltpu.SemaphoreType.DMA((count,)), pltpu.SemaphoreType.DMA((count,))]


M_ROWS, C_ROWS = 3 * H, 5 * H
M_PART, C_PART = M_ROWS // NY, C_ROWS // NY
EXCHANGES = (7, 7, 7, 7, 7, 7, 7, 7, 3, 7, 8)


def kernel(*refs):
    it = iter(refs)
    take = lambda n: [next(it) for _ in range(n)]
    (scale_ref,) = take(1)
    sources = take(10)
    (out_ref,) = take(1)
    targets = take(10)
    (copy_sems,) = take(1)
    sems = [take(2) for _ in EXCHANGES]
    z_ref, gv_ref, gr_ref, gg_ref, w_ref, v_ref, t2_ref, table_ref = take(8)
    mc_ref, gs_ref, m_ref, c_ref, m_in, c_in, g_in, g_sum, y_in = take(9)
    corr_ref, k_in, z_in, up_ref = take(4)
    elim = take(5)
    f_ref = elim[0]
    gk_ref, rk_ref, lk_ref, coords_ref, precision_ref, values_ref, sites_ref, prior_l, prior_r, prior_g = targets

    copies = [
        pltpu.make_async_copy(a, b, copy_sems.at[n]) for n, (a, b) in enumerate(zip(sources, targets))
    ]
    for copy in copies:
        copy.start()
    y, x, z, c = here()
    met = greet(
        [on_y(d) for d in range(1, NY)]
        + [on_xc(d) for d in GROUP]
        + [on_z(d) for d in range(1, NZ)]
    )
    for copy in copies[:6]:
        copy.wait()
    started = []

    scale = factors(scale_ref)
    knots = [upright(lk_ref[...]), upright(rk_ref[...]), upright(gk_ref[...])]
    scales = [scale[2], scale[1], scale[0]]
    gv_ref[...] = jnp.zeros_like(gv_ref)
    gr_ref[...] = jnp.zeros_like(gr_ref)
    gg_ref[...] = jnp.zeros_like(gg_ref)

    def step(i, _):
        at = pl.ds(pl.multiple_of(i * CHUNK, CHUNK), CHUNK)
        places = coords_ref[:, at]
        weight = jnp.sqrt(precision_ref[:, at])
        for n in range(3):
            z_ref[n * R : (n + 1) * R, :] = (basis(knots[n], places, scales[n]) * weight).astype(BF16)
        z_ref[3 * R :, :] = (values_ref[:, at].astype(F32) * weight).astype(BF16)
        gv_ref[...] += gram_of(z_ref[:R, :], z_ref[...])
        gr_ref[...] += gram_of(z_ref[R : 2 * R, :], z_ref[R:, :])
        gg_ref[...] += gram_of(z_ref[2 * R : 3 * R, :], z_ref[2 * R :, :])
        return 0

    lax.fori_loop(0, coords_ref.shape[1] // CHUNK, step, 0)
    for copy in copies[6:]:
        copy.wait()
    f_ref[...] = prior_l[...] + gv_ref[:, :R]
    eliminate(*elim[:1], w_ref, v_ref, *elim[1:])

    def scatter(rows, first, part, target, pair):
        copies = []
        for d in range(1, NY):
            place = on_y(d)
            at = pl.ds(pl.multiple_of(first + place[0] * part, 8), part)
            copies.append(send(rows.at[at, :], target.at[d - 1], pair, d - 1, place))
        started.extend(copies)
        return copies

    def gather(ref, part, pair):
        at = pl.ds(pl.multiple_of(y * part, 8), part)
        copies = [send(ref.at[at, :], ref.at[at, :], pair, d - 1, on_y(d)) for d in range(1, NY)]
        started.extend(copies)
        return copies

    t1 = dot(w_ref[...], gv_ref[:, R : 2 * R])
    t2_ref[:, :R] = dot(v_ref[...], gv_ref[:, R : 2 * R])
    regional = gr_ref[:, :R] - dot_t(t1, t2_ref[:, :R])
    mc_ref[0:H, :] = regional[:H, :H]
    mc_ref[H : 2 * H, :] = regional[H:, :H]
    mc_ref[2 * H : 3 * H, :] = regional[H:, H:R]
    met()
    m_scatter = scatter(mc_ref, 0, M_PART, m_in, sems[0])
    t2_ref[:, R:] = dot(v_ref[...], gv_ref[:, 2 * R :])
    regional = gr_ref[:, R:] - dot_t(t1, t2_ref[:, R:])
    for r in range(2):
        for n in range(2):
            k = 3 + 2 * r + n
            mc_ref[k * H : (k + 1) * H, :] = regional[r * H : (r + 1) * H, n * H : (n + 1) * H]
    mc_ref[7 * H :, :] = jnp.concatenate([regional[:H, R:], regional[H:, R:]], axis=1)
    t1 = dot(w_ref[...], gv_ref[:, 2 * R : 3 * R])
    pack_global(gs_ref, gg_ref[...] - dot_t(t1, t2_ref[:, R:]))
    g_scatter = []
    for n, d in enumerate(GROUP):
        place = on_xc(d)
        g_scatter.append(send(gs_ref.at[place[3], :, place[1]], g_in.at[n], sems[1], n, place))
    started.extend(g_scatter)
    arrived(m_scatter)
    own = pl.ds(pl.multiple_of(y * M_PART, 8), M_PART)
    m_ref[own, :] = added(mc_ref[own, :], m_in)
    m_gather = gather(m_ref, M_PART, sems[2])
    c_scatter = scatter(mc_ref, M_ROWS, C_PART, c_in, sems[3])

    places = sites_ref[...]
    sites_l = dot(w_ref[...], basis(knots[0], places, scales[0]))
    seen = dot_t(t2_ref[...], sites_l)
    table_ref[:R, :] = basis(knots[1], places, scales[1]) - seen[:R]
    table_ref[R : 2 * R, :] = basis(knots[2], places, scales[2]) - seen[R : 2 * R]
    table_ref[2 * R :, :] = seen[2 * R :]

    arrived(m_gather)
    f_ref[...] = prior_r[...] + whole_of(m_ref, 0)
    later = {}

    def between():
        arrived(c_scatter)
        mine = pl.ds(pl.multiple_of(y * C_PART, 8), C_PART)
        theirs = pl.ds(pl.multiple_of(M_ROWS + y * C_PART, 8), C_PART)
        c_ref[mine, :] = added(mc_ref[theirs, :], c_in)
        later["c"] = gather(c_ref, C_PART, sems[4])
        arrived(g_scatter)
        g_sum[...] = added(gs_ref[c, :, x], g_in)
        later["y"] = []
        for d in range(1, NY):
            place = on_y(d)
            later["y"].append(send(g_sum.at[place[0]], y_in.at[d - 1], sems[5], d - 1, place))
        started.extend(later["y"])

    eliminate(*elim[:1], w_ref, v_ref, *elim[1:], between=between)
    arrived(later["c"])
    cross = jnp.concatenate(
        [
            jnp.concatenate([c_ref[(2 * r + n) * H : (2 * r + n + 1) * H, :] for n in range(2)], axis=1)
            for r in range(2)
        ],
        axis=0,
    )
    t1 = dot(w_ref[...], cross)
    t2_ref[:, : R + FIELDS] = dot(v_ref[...], jnp.concatenate([cross, fields_of(c_ref, 4)], axis=1))
    pack_global(corr_ref, dot_t(t1, t2_ref[:, : R + FIELDS]))

    first = []
    for n, d in enumerate(GROUP):
        place = on_xc(d)
        first.append(send(corr_ref.at[place[3], y, place[1]], k_in.at[n], sems[6], n, place))
    arrived(later["y"])
    share = added(g_sum[y], y_in)
    arrived(first)
    z_in[z] = share - added(corr_ref[c, y, x], k_in)
    second = [send(z_in.at[z], z_in.at[z], sems[7], d - 1, on_z(d)) for d in range(1, NZ)]
    sites_r = dot(w_ref[...], table_ref[:R, :])
    seen = dot_t(t2_ref[:, : R + FIELDS], sites_r)
    table_ref[R : 2 * R, :] -= seen[:R]
    table_ref[2 * R :, :] += seen[R:]
    arrived(second)
    up_ref[c, y, x] = total_of([z_in[n] for n in range(NZ)])
    third = [
        send(up_ref.at[c, y, x], up_ref.at[c, y, x], sems[8], dx - 1, on_xc((dx, 0)))
        for dx in range(1, NX)
    ]
    arrived(third)
    fourth = [send(up_ref.at[c, y], up_ref.at[c, y], sems[9], d - 1, on_y(d)) for d in range(1, NY)]
    fifth = [send(up_ref.at[c, y], up_ref.at[c, y], sems[10], 0, on_xc((0, 1)))]
    for d in range(1, NY):
        fourth[d - 1].wait_recv()
        block = up_ref.at[c, lax.rem(y - d + NY, NY)]
        fifth.append(send(block, block, sems[10], d, on_xc((0, 1))))
    arrived(fifth)
    upper = up_ref[...].reshape(4 * H, H)
    f_ref[...] = prior_g[...] + whole_of(upper, 0)
    eliminate(*elim[:1], w_ref, v_ref, *elim[1:])
    g = dot_t(w_ref[...], dot(v_ref[...], fields_of(upper, 3)))
    out_ref[...] = table_ref[2 * R :, :] + dot_t(g, table_ref[R : 2 * R, :])
    sent(started + first + second + third + fourth + fifth)


def everything(scales, *operands):
    sites = operands[6]
    sems = []
    for count in EXCHANGES:
        sems += pair_of_sems(count)
    tiles = pltpu.VMEM((NC, NY, NX, B, H), F32)
    return pl.pallas_call(
        kernel,
        name="all",
        out_shape=shape(FIELDS, sites.shape[1]),
        in_specs=[SMEM] + [pl.BlockSpec(memory_space=pl.ANY)] * len(operands),
        out_specs=VMEM,
        scratch_shapes=[pltpu.VMEM(a.shape, a.dtype) for a in operands]
        + [pltpu.SemaphoreType.DMA((len(operands),))]
        + sems
        + [
            pltpu.VMEM((3 * R + FIELDS, CHUNK), BF16),
            pltpu.VMEM((R, 3 * R + FIELDS), F32),
            pltpu.VMEM((R, 2 * R + FIELDS), F32),
            pltpu.VMEM((R, R + FIELDS), F32),
            pltpu.VMEM((R, R), F32),
            pltpu.VMEM((R, R), F32),
            pltpu.VMEM((R, 2 * R + FIELDS), F32),
            pltpu.VMEM((2 * R + FIELDS, sites.shape[1]), F32),
            pltpu.VMEM((8 * H, H), F32),
            tiles,
            pltpu.VMEM((M_ROWS, H), F32),
            pltpu.VMEM((C_ROWS, H), F32),
            pltpu.VMEM((NY - 1, M_PART, H), F32),
            pltpu.VMEM((NY - 1, C_PART, H), F32),
            pltpu.VMEM((7, NY, B, H), F32),
            pltpu.VMEM((NY, B, H), F32),
            pltpu.VMEM((NY - 1, B, H), F32),
            tiles,
            pltpu.VMEM((7, B, H), F32),
            pltpu.VMEM((NZ, B, H), F32),
            tiles,
        ]
        + eliminate_scratch(),
        compiler_params=pltpu.CompilerParams(
            vmem_limit_bytes=LIMIT, collective_id=0, has_side_effects=True
        ),
    )(scales, *operands)


def shards(
    obs_coords,
    obs_values,
    obs_precision,
    site_coords,
    length_scale,
    global_knots,
    region_knots,
    leaf_knots,
    global_prior,
    region_prior,
    leaf_prior,
):
    return everything(
        length_scale,
        global_knots,
        region_knots[0],
        leaf_knots[0],
        obs_coords,
        obs_precision[None],
        obs_values,
        site_coords,
        leaf_prior[0],
        region_prior[0],
        global_prior,
    )


def solution(mesh):
    split = Mesh(
        mesh.devices.reshape(NY, NX, NZ, NC),
        ("region", "super_0", "super_1", "super_2"),
    )
    return jax.shard_map(
        shards,
        mesh=split,
        in_specs=(
            P(None, REGION_SUPER),
            P(None, REGION_SUPER),
            P(REGION_SUPER),
            P(None, REGION_SUPER),
            P(),
            P(),
            P(SUPER, None, None),
            P(REGION_SUPER, None, None),
            P(),
            P(SUPER, None, None),
            P(REGION_SUPER, None, None),
        ),
        out_specs=P(None, REGION_SUPER),
        check_vma=False,
    )
```

```python
import functools

import jax
import jax.numpy as jnp
from jax import lax
from jax.experimental import pallas as pl
from jax.experimental.pallas import tpu as pltpu
from jax.sharding import Mesh
from jax.sharding import PartitionSpec as P

R = 256
B = 8
H = 128
FIELDS = 64
F32 = jnp.float32
BF16 = jnp.bfloat16
HIGH = lax.Precision.HIGHEST
MESH = pl.DeviceIdType.MESH
REGION_SUPER = ("region", "super_0", "super_1", "super_2")
SUPER = ("super_0", "super_1", "super_2")
VMEM = pl.BlockSpec(memory_space=pltpu.VMEM)
SMEM = pl.BlockSpec(memory_space=pltpu.SMEM)
LIMIT = 60 * 1024 * 1024


def parts_of(x):
    high = x.astype(BF16).astype(F32)
    rest = x - high
    middle = rest.astype(BF16).astype(F32)
    return high, middle, rest - middle


def left_stack(x):
    h, m, l = parts_of(x)
    return jnp.concatenate([h, h, m, h, l, m], axis=0).astype(BF16)


def right_stack(x):
    h, m, l = parts_of(x)
    return jnp.concatenate([h, m, h, l, h, m], axis=0).astype(BF16)


def total_of(terms):
    terms = list(terms)
    while len(terms) > 1:
        pairs = [terms[i] + terms[i + 1] for i in range(0, len(terms) - 1, 2)]
        terms = pairs + terms[len(pairs) * 2 :]
    return terms[0]


def columns_of(x, first):
    zero = jnp.zeros((B, H), jnp.int32)
    return [jnp.take_along_axis(x, zero + (first + j), axis=1) for j in range(B)]


def row_of(ref, r):
    return jnp.broadcast_to(ref[r : r + 1, :], (B, ref.shape[1]))


def twice(x):
    return jnp.concatenate([x, x], axis=1)


def eliminate(f_ref, w_ref, v_ref, cols_ref, rows_ref, mine_ref, x_ref, lh_ref, xh_ref, hooks=()):
    lane = lax.broadcasted_iota(jnp.int32, (B, R), 1)
    sub = lax.broadcasted_iota(jnp.int32, (B, R), 0)
    sub_half = lax.broadcasted_iota(jnp.int32, (B, H), 0)
    for ref in (mine_ref, x_ref, lh_ref, xh_ref):
        ref[...] = jnp.zeros_like(ref)

    def body(first, k, panel):
        base = pl.multiple_of(k * B, B)
        half = lax.div(k, 16)
        at = (k - 16 * half) * B
        diag = jnp.where(half == 0, panel[:, :H], panel[:, H:])
        for j, column in enumerate(columns_of(diag, at)):
            cols_ref[j * B : (j + 1) * B, :] = column
        mark = (lane >= base) & (lane < base + B)
        eye = jnp.where(lane == base + sub, 1.0, 0.0).astype(F32)
        rows_ref[...] = jnp.where(mark, eye, panel)
        following = pl.multiple_of(jnp.minimum(k + 1, R // B - 1) * B, B)
        ahead = f_ref[pl.ds(following, B), :]
        next_half = lax.div(following, H)
        next_at = following - next_half * H + sub_half

        def upright_of(row):
            part = jnp.where(next_half == 0, row[:, :H], row[:, H:])
            return jnp.take_along_axis(part, next_at, axis=1)

        keep = jnp.where((lane >= base - B) & (lane < base), 0.0, 1.0).astype(F32)
        before = [upright_of(row_of(mine_ref, j)) for j in range(B)]
        ahead = ahead * keep - total_of([twice(before[j]) * row_of(x_ref, j) for j in range(B)])
        f_ref[first:, :] = f_ref[first:, :] * keep[0:1, :] - lax.dot_general(
            lh_ref[:, first:], xh_ref[...], (((0,), (0,)), ((), ())), preferred_element_type=F32
        )
        rows = [row_of(rows_ref, j) for j in range(B)]
        g = [upright_of(row) for row in rows]
        s = {}
        for j in range(B):
            for i in range(j + 1):
                s[i, j] = row_of(cols_ref, j * B + i)
        low = {}
        inv = []
        for p in range(B):
            inv.append(1.0 / s[p, p])
            for i in range(p + 1, B):
                m = s[p, i] * inv[p]
                for j in range(i, B):
                    s[i, j] = s[i, j] - m * s[p, j]
                for c in range(p):
                    low[i, c] = low[i, c] - m * low[p, c]
                low[i, p] = -m
        row = [total_of([twice(low[j, m]) * rows[m] for m in range(j)] + [rows[j]]) for j in range(B)]
        lcol = [total_of([g[m] * low[j, m] for m in range(j)] + [g[j]]) * inv[j] for j in range(B)]
        panel_next = jnp.where(mark, 0.0, ahead) - total_of([twice(lcol[j]) * row[j] for j in range(B)])
        dcol = inv[0]
        mine = row[0]
        for i in range(1, B):
            dcol = jnp.where(sub_half == i, inv[i], dcol)
            mine = jnp.where(sub == i, row[i], mine)
        x = twice(dcol) * mine
        done = lane < base + B
        w_ref[pl.ds(base, B), :] = jnp.where(done, mine, 0.0)
        v_ref[pl.ds(base, B), :] = jnp.where(done, x, 0.0)
        mine_ref[...] = mine
        x_ref[...] = x
        lh_ref[...] = left_stack(jnp.where(done, 0.0, mine))
        xh_ref[...] = right_stack(x)
        return panel_next

    panel = f_ref[0:B, :]
    at = 0
    for stop, hook in sorted([*hooks, (R // B // 2, None), (R // B, None)], key=lambda h: h[0]):
        if stop > at:
            first = H if at >= R // B // 2 else 0
            panel = lax.fori_loop(at, stop, functools.partial(body, first), panel)
            at = stop
        if hook is not None:
            hook()


def eliminate_scratch():
    return [
        pltpu.VMEM((R, R), F32),
        pltpu.VMEM((B * B, H), F32),
        pltpu.VMEM((B, R), F32),
        pltpu.VMEM((B, R), F32),
        pltpu.VMEM((B, R), F32),
        pltpu.VMEM((48, R), BF16),
        pltpu.VMEM((48, R), BF16),
    ]


def dot(a, b):
    return jnp.dot(a, b, precision=HIGH, preferred_element_type=F32)


def dot_t(a, b):
    return lax.dot_general(a, b, (((0,), (0,)), ((), ())), precision=HIGH, preferred_element_type=F32)


def gram_of(a, b):
    return lax.dot_general(a, b, (((1,), (1,)), ((), ())), preferred_element_type=F32)


def upright(knots):
    spare = jnp.zeros((6, R), F32)
    return jnp.concatenate([knots, spare], axis=0).T


def basis(knots, places, scale):
    diff_x = knots[:, 0:1] - places[0:1, :]
    diff_y = knots[:, 1:2] - places[1:2, :]
    return jnp.exp((diff_x * diff_x + diff_y * diff_y) * scale)


def factors(scale_ref):
    return [-0.5 / (scale_ref[i] * scale_ref[i]) for i in range(3)]


CHUNK = 1024


def pack_global(out_ref, upper):
    rows = [
        upper[:H, :H],
        upper[H:, :H],
        upper[H:, H:R],
        jnp.concatenate([upper[:H, R:], upper[H:, R:]], axis=1),
    ]
    out_ref[...] = jnp.concatenate(rows, axis=0).reshape(out_ref.shape)


def whole_of(ref, first):
    a, b, c = (ref[(first + n) * H : (first + n + 1) * H, :] for n in range(3))
    return jnp.concatenate(
        [jnp.concatenate([a, b.T], axis=1), jnp.concatenate([b, c], axis=1)], axis=0
    )


def fields_of(ref, block):
    y = ref[block * H : (block + 1) * H, :]
    return jnp.concatenate([y[:, :FIELDS], y[:, FIELDS:]], axis=0)


def shape(*dims):
    return jax.ShapeDtypeStruct(dims, F32)


NY, NX, NZ, NC = 8, 4, 8, 2
GROUP = [(dx, dc) for dx in range(NX) for dc in range(NC)][1:]
NEAREST = sorted(range(NY), key=lambda d: min(d, NY - d))
PLANE = [(dx, dy) for dy in NEAREST[::-1] for dx in range(NX) if (dx, dy) != (0, 0)]


def here():
    return (
        lax.axis_index("region"),
        lax.axis_index("super_0"),
        lax.axis_index("super_1"),
        lax.axis_index("super_2"),
    )


def on_y(d):
    y, x, z, c = here()
    return (lax.rem(y + d, NY), x, z, c)


def on_z(d):
    y, x, z, c = here()
    return (y, x, lax.rem(z + d, NZ), c)


def on_xc(d):
    y, x, z, c = here()
    return (y, lax.rem(x + d[0], NX), z, lax.rem(c + d[1], NC))


def on_xy(d):
    y, x, z, c = here()
    return (lax.rem(y + d[1], NY), lax.rem(x + d[0], NX), z, c)


def greet(places):
    barrier = pltpu.get_barrier_semaphore()
    for place in places:
        pl.semaphore_signal(barrier, inc=1, device_id=place, device_id_type=MESH)
    return lambda: pl.semaphore_wait(barrier, len(places))


def send(source, target, sems, n, place):
    copy = pltpu.make_async_remote_copy(
        src_ref=source,
        dst_ref=target,
        send_sem=sems[0].at[n],
        recv_sem=sems[1].at[n],
        device_id=place,
        device_id_type=MESH,
    )
    copy.start()
    return copy


def arrived(copies):
    for copy in copies:
        copy.wait_recv()


def sent(copies):
    for copy in copies:
        copy.wait_send()


def added(own, arrivals_ref):
    return total_of([own] + [arrivals_ref[n] for n in range(arrivals_ref.shape[0])])


def pair_of_sems(count):
    return [pltpu.SemaphoreType.DMA((count,)), pltpu.SemaphoreType.DMA((count,))]


M_ROWS, C_ROWS = 3 * H, 5 * H
M_PART, C_PART = M_ROWS // NY, C_ROWS // NY
EXCHANGES = (7, 7, 7, 7, 7, 7, 7, 7, 31, 8)
CROSS_STEP = 0


def kernel(*refs):
    it = iter(refs)
    take = lambda n: [next(it) for _ in range(n)]
    (scale_ref,) = take(1)
    sources = take(10)
    (out_ref,) = take(1)
    targets = take(10)
    (copy_sems,) = take(1)
    sems = [take(2) for _ in EXCHANGES]
    z_refs = take(2)
    gv_ref, gr_ref, gg_ref, w_ref, v_ref, t2_ref, table_ref = take(7)
    mc_ref, gs_ref, m_ref, c_ref, m_in, c_in, g_in, g_sum, y_in = take(9)
    corr_ref, k_in, z_in, up_ref = take(4)
    elim = take(7)
    f_ref = elim[0]
    gk_ref, rk_ref, lk_ref, coords_ref, precision_ref, values_ref, sites_ref, prior_l, prior_r, prior_g = targets

    copies = [
        pltpu.make_async_copy(a, b, copy_sems.at[n]) for n, (a, b) in enumerate(zip(sources, targets))
    ]
    for copy in copies:
        copy.start()
    y, x, z, c = here()
    met = greet(
        [on_xy(d) for d in PLANE]
        + [on_xc(d) for d in GROUP if d[1]]
        + [on_z(d) for d in range(1, NZ)]
    )
    for copy in copies[:6]:
        copy.wait()
    started = []

    scale = factors(scale_ref)
    knots = [upright(lk_ref[...]), upright(rk_ref[...]), upright(gk_ref[...])]
    scales = [scale[2], scale[1], scale[0]]
    grams = (gv_ref, gr_ref, gg_ref)
    chunks = coords_ref.shape[1] // CHUNK

    def fill(z_ref, i):
        at = pl.ds(i * CHUNK, CHUNK)
        places = coords_ref[:, at]
        weight = jnp.sqrt(precision_ref[:, at])
        z_ref[:FIELDS, :] = (values_ref[:, at].astype(F32) * weight).astype(BF16)
        for n in range(3):
            first = FIELDS + n * R
            z_ref[first : first + R, :] = (basis(knots[n], places, scales[n]) * weight).astype(BF16)

    fill(z_refs[0], 0)
    for i in range(chunks):
        now, later = z_refs[i % 2], z_refs[(i + 1) % 2]
        if i + 1 < chunks:
            fill(later, i + 1)
        for n, ref in enumerate(grams):
            first = FIELDS + n * R
            block = gram_of(now[: first + R, :], now[first : first + R, :])
            ref[...] = block if i == 0 else ref[...] + block
    for copy in copies[6:]:
        copy.wait()
    f_ref[...] = prior_l[...] + gv_ref[FIELDS:, :]
    eliminate(*elim[:1], w_ref, v_ref, *elim[1:])

    def scatter(rows, first, part, target, pair):
        copies = []
        for d in range(1, NY):
            place = on_y(d)
            at = pl.ds(pl.multiple_of(first + place[0] * part, 8), part)
            copies.append(send(rows.at[at, :], target.at[d - 1], pair, d - 1, place))
        started.extend(copies)
        return copies

    def gather(ref, part, pair):
        at = pl.ds(pl.multiple_of(y * part, 8), part)
        copies = [send(ref.at[at, :], ref.at[at, :], pair, d - 1, on_y(d)) for d in range(1, NY)]
        started.extend(copies)
        return copies

    leaf_rows = slice(FIELDS, FIELDS + R)
    region_rows = slice(FIELDS + R, FIELDS + 2 * R)
    t1 = dot(w_ref[...], gr_ref[leaf_rows, :])
    t2_ref[:, :R] = dot(v_ref[...], gr_ref[leaf_rows, :])
    regional = gr_ref[region_rows, :] - dot_t(t1, t2_ref[:, :R])
    mc_ref[0:H, :] = regional[:H, :H]
    mc_ref[H : 2 * H, :] = regional[H:, :H]
    mc_ref[2 * H : 3 * H, :] = regional[H:, H:R]
    met()
    m_scatter = scatter(mc_ref, 0, M_PART, m_in, sems[0])
    right = jnp.concatenate([gg_ref[leaf_rows, :], gv_ref[:FIELDS, :].T], axis=1)
    t2_ref[:, R:] = dot(v_ref[...], right)
    regional = jnp.concatenate([gg_ref[region_rows, :], gr_ref[:FIELDS, :].T], axis=1) - dot_t(
        t1, t2_ref[:, R:]
    )
    for r in range(2):
        for n in range(2):
            k = 3 + 2 * r + n
            mc_ref[k * H : (k + 1) * H, :] = regional[r * H : (r + 1) * H, n * H : (n + 1) * H]
    mc_ref[7 * H :, :] = jnp.concatenate([regional[:H, R:], regional[H:, R:]], axis=1)
    c_scatter = scatter(mc_ref, M_ROWS, C_PART, c_in, sems[3])
    t1 = dot(w_ref[...], gg_ref[leaf_rows, :])
    upper = jnp.concatenate([gg_ref[FIELDS + 2 * R :, :], gg_ref[:FIELDS, :].T], axis=1)
    pack_global(gs_ref, upper - dot_t(t1, t2_ref[:, R:]))
    g_scatter = []
    for n, d in enumerate(GROUP):
        place = on_xc(d)
        g_scatter.append(send(gs_ref.at[place[3], :, place[1]], g_in.at[n], sems[1], n, place))
    started.extend(g_scatter)
    arrived(m_scatter)
    own = pl.ds(pl.multiple_of(y * M_PART, 8), M_PART)
    m_ref[own, :] = added(mc_ref[own, :], m_in)
    m_gather = gather(m_ref, M_PART, sems[2])

    places = sites_ref[...]
    sites_l = dot(w_ref[...], basis(knots[0], places, scales[0]))
    seen = dot_t(t2_ref[...], sites_l)
    table_ref[:R, :] = basis(knots[1], places, scales[1]) - seen[:R]
    table_ref[R : 2 * R, :] = basis(knots[2], places, scales[2]) - seen[R : 2 * R]
    table_ref[2 * R :, :] = seen[2 * R :]

    arrived(m_gather)
    f_ref[...] = prior_r[...] + whole_of(m_ref, 0)
    later = {}

    def send_cross():
        arrived(c_scatter)
        mine = pl.ds(pl.multiple_of(y * C_PART, 8), C_PART)
        theirs = pl.ds(pl.multiple_of(M_ROWS + y * C_PART, 8), C_PART)
        c_ref[mine, :] = added(mc_ref[theirs, :], c_in)
        later["c"] = gather(c_ref, C_PART, sems[4])

    def send_share():
        arrived(g_scatter)
        g_sum[...] = added(gs_ref[c, :, x], g_in)
        later["y"] = []
        for d in range(1, NY):
            place = on_y(d)
            later["y"].append(send(g_sum.at[place[0]], y_in.at[d - 1], sems[5], d - 1, place))
        started.extend(later["y"])

    eliminate(*elim[:1], w_ref, v_ref, *elim[1:], hooks=[(CROSS_STEP, send_cross), (20, send_share)])
    arrived(later["c"])
    cross = jnp.concatenate(
        [
            jnp.concatenate([c_ref[(2 * r + n) * H : (2 * r + n + 1) * H, :] for n in range(2)], axis=1)
            for r in range(2)
        ],
        axis=0,
    )
    t1 = dot(w_ref[...], cross)
    t2_ref[:, : R + FIELDS] = dot(v_ref[...], jnp.concatenate([cross, fields_of(c_ref, 4)], axis=1))
    pack_global(corr_ref, dot_t(t1, t2_ref[:, : R + FIELDS]))

    first = []
    for n, d in enumerate(GROUP):
        place = on_xc(d)
        first.append(send(corr_ref.at[place[3], y, place[1]], k_in.at[n], sems[6], n, place))
    arrived(later["y"])
    share = added(g_sum[y], y_in)
    arrived(first)
    z_in[z] = share - added(corr_ref[c, y, x], k_in)
    second = [send(z_in.at[z], z_in.at[z], sems[7], d - 1, on_z(d)) for d in range(1, NZ)]
    sites_r = dot(w_ref[...], table_ref[:R, :])
    seen = dot_t(t2_ref[:, : R + FIELDS], sites_r)
    table_ref[R : 2 * R, :] -= seen[:R]
    table_ref[2 * R :, :] += seen[R:]
    arrived(second)
    up_ref[c, y, x] = total_of([z_in[n] for n in range(NZ)])
    third = {}
    for n, d in enumerate(PLANE):
        third[d] = send(up_ref.at[c, y, x], up_ref.at[c, y, x], sems[8], n, on_xy(d))
    fourth = []
    for dy in NEAREST:
        for dx in range(NX):
            if (dx, dy) != (0, 0):
                third[dx, dy].wait_recv()
        block = up_ref.at[c, lax.rem(y - dy + NY, NY)]
        fourth.append(send(block, block, sems[9], dy, on_xc((0, 1))))
    arrived(fourth)
    upper = up_ref[...].reshape(4 * H, H)
    f_ref[...] = prior_g[...] + whole_of(upper, 0)
    eliminate(*elim[:1], w_ref, v_ref, *elim[1:])
    g = dot_t(w_ref[...], dot(v_ref[...], fields_of(upper, 3)))
    out_ref[...] = table_ref[2 * R :, :] + dot_t(g, table_ref[R : 2 * R, :])
    sent(started + first + second + list(third.values()) + fourth)


def everything(scales, *operands):
    sites = operands[6]
    sems = []
    for count in EXCHANGES:
        sems += pair_of_sems(count)
    tiles = pltpu.VMEM((NC, NY, NX, B, H), F32)
    return pl.pallas_call(
        kernel,
        name="all",
        out_shape=shape(FIELDS, sites.shape[1]),
        in_specs=[SMEM] + [pl.BlockSpec(memory_space=pl.ANY)] * len(operands),
        out_specs=VMEM,
        scratch_shapes=[pltpu.VMEM(a.shape, a.dtype) for a in operands]
        + [pltpu.SemaphoreType.DMA((len(operands),))]
        + sems
        + [
            pltpu.VMEM((3 * R + FIELDS, CHUNK), BF16),
            pltpu.VMEM((3 * R + FIELDS, CHUNK), BF16),
            pltpu.VMEM((FIELDS + R, R), F32),
            pltpu.VMEM((FIELDS + 2 * R, R), F32),
            pltpu.VMEM((FIELDS + 3 * R, R), F32),
            pltpu.VMEM((R, R), F32),
            pltpu.VMEM((R, R), F32),
            pltpu.VMEM((R, 2 * R + FIELDS), F32),
            pltpu.VMEM((2 * R + FIELDS, sites.shape[1]), F32),
            pltpu.VMEM((8 * H, H), F32),
            tiles,
            pltpu.VMEM((M_ROWS, H), F32),
            pltpu.VMEM((C_ROWS, H), F32),
            pltpu.VMEM((NY - 1, M_PART, H), F32),
            pltpu.VMEM((NY - 1, C_PART, H), F32),
            pltpu.VMEM((7, NY, B, H), F32),
            pltpu.VMEM((NY, B, H), F32),
            pltpu.VMEM((NY - 1, B, H), F32),
            tiles,
            pltpu.VMEM((7, B, H), F32),
            pltpu.VMEM((NZ, B, H), F32),
            tiles,
        ]
        + eliminate_scratch(),
        compiler_params=pltpu.CompilerParams(
            vmem_limit_bytes=LIMIT, collective_id=0, has_side_effects=True
        ),
    )(scales, *operands)


def shards(
    obs_coords,
    obs_values,
    obs_precision,
    site_coords,
    length_scale,
    global_knots,
    region_knots,
    leaf_knots,
    global_prior,
    region_prior,
    leaf_prior,
):
    return everything(
        length_scale,
        global_knots,
        region_knots[0],
        leaf_knots[0],
        obs_coords,
        obs_precision[None],
        obs_values,
        site_coords,
        leaf_prior[0],
        region_prior[0],
        global_prior,
    )


def solution(mesh):
    split = Mesh(
        mesh.devices.reshape(NY, NX, NZ, NC),
        ("region", "super_0", "super_1", "super_2"),
    )
    return jax.shard_map(
        shards,
        mesh=split,
        in_specs=(
            P(None, REGION_SUPER),
            P(None, REGION_SUPER),
            P(REGION_SUPER),
            P(None, REGION_SUPER),
            P(),
            P(),
            P(SUPER, None, None),
            P(REGION_SUPER, None, None),
            P(),
            P(SUPER, None, None),
            P(REGION_SUPER, None, None),
        ),
        out_specs=P(None, REGION_SUPER),
        check_vma=False,
    )
```

```python
import functools

import jax
import jax.numpy as jnp
from jax import lax
from jax.experimental import pallas as pl
from jax.experimental.pallas import tpu as pltpu
from jax.sharding import Mesh
from jax.sharding import PartitionSpec as P

R = 256
B = 8
H = 128
FIELDS = 64
F32 = jnp.float32
BF16 = jnp.bfloat16
HIGH = lax.Precision.HIGHEST
MESH = pl.DeviceIdType.MESH
REGION_SUPER = ("region", "super_0", "super_1", "super_2")
SUPER = ("super_0", "super_1", "super_2")
VMEM = pl.BlockSpec(memory_space=pltpu.VMEM)
SMEM = pl.BlockSpec(memory_space=pltpu.SMEM)
LIMIT = 60 * 1024 * 1024


def parts_of(x):
    high = x.astype(BF16).astype(F32)
    rest = x - high
    middle = rest.astype(BF16).astype(F32)
    return high, middle, rest - middle


def left_stack(x):
    h, m, l = parts_of(x)
    return jnp.concatenate([h, h, m, h, l, m], axis=0).astype(BF16)


def right_stack(x):
    h, m, l = parts_of(x)
    return jnp.concatenate([h, m, h, l, h, m], axis=0).astype(BF16)


def total_of(terms):
    terms = list(terms)
    while len(terms) > 1:
        pairs = [terms[i] + terms[i + 1] for i in range(0, len(terms) - 1, 2)]
        terms = pairs + terms[len(pairs) * 2 :]
    return terms[0]


def columns_of(x, first):
    zero = jnp.zeros((B, H), jnp.int32)
    return [jnp.take_along_axis(x, zero + (first + j), axis=1) for j in range(B)]


def row_of(ref, r):
    return jnp.broadcast_to(ref[r : r + 1, :], (B, ref.shape[1]))


def twice(x):
    return jnp.concatenate([x, x], axis=1)


def eliminate(f_ref, w_ref, d_ref, cols_ref, rows_ref, mine_ref, x_ref, lh_ref, xh_ref, hooks=()):
    lane = lax.broadcasted_iota(jnp.int32, (B, R), 1)
    sub = lax.broadcasted_iota(jnp.int32, (B, R), 0)
    sub_half = lax.broadcasted_iota(jnp.int32, (B, H), 0)
    for ref in (mine_ref, x_ref, lh_ref, xh_ref):
        ref[...] = jnp.zeros_like(ref)

    def body(first, k, panel):
        base = pl.multiple_of(k * B, B)
        half = lax.div(k, 16)
        at = (k - 16 * half) * B
        diag = jnp.where(half == 0, panel[:, :H], panel[:, H:])
        for j, column in enumerate(columns_of(diag, at)):
            cols_ref[j * B : (j + 1) * B, :] = column
        mark = (lane >= base) & (lane < base + B)
        eye = jnp.where(lane == base + sub, 1.0, 0.0).astype(F32)
        rows_ref[...] = jnp.where(mark, eye, panel)
        following = pl.multiple_of(jnp.minimum(k + 1, R // B - 1) * B, B)
        ahead = f_ref[pl.ds(following, B), :]
        next_half = lax.div(following, H)
        next_at = following - next_half * H + sub_half

        def upright_of(row):
            part = jnp.where(next_half == 0, row[:, :H], row[:, H:])
            return jnp.take_along_axis(part, next_at, axis=1)

        keep = jnp.where((lane >= base - B) & (lane < base), 0.0, 1.0).astype(F32)
        before = [upright_of(row_of(mine_ref, j)) for j in range(B)]
        ahead = ahead * keep - total_of([twice(before[j]) * row_of(x_ref, j) for j in range(B)])
        f_ref[first:, :] = f_ref[first:, :] * keep[0:1, :] - lax.dot_general(
            lh_ref[:, first:], xh_ref[...], (((0,), (0,)), ((), ())), preferred_element_type=F32
        )
        rows = [row_of(rows_ref, j) for j in range(B)]
        g = [upright_of(row) for row in rows]
        s = {}
        for j in range(B):
            for i in range(j + 1):
                s[i, j] = row_of(cols_ref, j * B + i)
        low = {}
        inv = []
        for p in range(B):
            inv.append(1.0 / s[p, p])
            for i in range(p + 1, B):
                m = s[p, i] * inv[p]
                for j in range(i, B):
                    s[i, j] = s[i, j] - m * s[p, j]
                for c in range(p):
                    low[i, c] = low[i, c] - m * low[p, c]
                low[i, p] = -m
        row = [total_of([twice(low[j, m]) * rows[m] for m in range(j)] + [rows[j]]) for j in range(B)]
        lcol = [total_of([g[m] * low[j, m] for m in range(j)] + [g[j]]) * inv[j] for j in range(B)]
        panel_next = jnp.where(mark, 0.0, ahead) - total_of([twice(lcol[j]) * row[j] for j in range(B)])
        dcol = inv[0]
        mine = row[0]
        for i in range(1, B):
            dcol = jnp.where(sub_half == i, inv[i], dcol)
            mine = jnp.where(sub == i, row[i], mine)
        x = twice(dcol) * mine
        done = lane < base + B
        w_ref[pl.ds(base, B), :] = jnp.where(done, mine, 0.0)
        d_ref[pl.ds(base, B), :] = dcol
        mine_ref[...] = mine
        x_ref[...] = x
        lh_ref[...] = left_stack(jnp.where(done, 0.0, mine))
        xh_ref[...] = right_stack(x)
        return panel_next

    panel = f_ref[0:B, :]
    at = 0
    for stop, hook in sorted([*hooks, (R // B // 2, None), (R // B, None)], key=lambda h: h[0]):
        if stop > at:
            first = H if at >= R // B // 2 else 0
            panel = lax.fori_loop(at, stop, functools.partial(body, first), panel)
            at = stop
        if hook is not None:
            hook()


def eliminate_scratch():
    return [
        pltpu.VMEM((R, R), F32),
        pltpu.VMEM((B * B, H), F32),
        pltpu.VMEM((B, R), F32),
        pltpu.VMEM((B, R), F32),
        pltpu.VMEM((B, R), F32),
        pltpu.VMEM((48, R), BF16),
        pltpu.VMEM((48, R), BF16),
    ]


def dot(a, b):
    return jnp.dot(a, b, precision=HIGH, preferred_element_type=F32)


def dot_t(a, b):
    return lax.dot_general(a, b, (((0,), (0,)), ((), ())), precision=HIGH, preferred_element_type=F32)


def scaled(t, d_ref):
    whole, rest = divmod(t.shape[1], H)
    d = d_ref[...]
    return t * jnp.concatenate([d] * whole + [d[:, :rest]] * (rest > 0), axis=1)


def gram_of(a, b):
    return lax.dot_general(a, b, (((1,), (1,)), ((), ())), preferred_element_type=F32)


def upright(knots):
    spare = jnp.zeros((6, R), F32)
    return jnp.concatenate([knots, spare], axis=0).T


def basis(knots, places, scale):
    diff_x = knots[:, 0:1] - places[0:1, :]
    diff_y = knots[:, 1:2] - places[1:2, :]
    return jnp.exp((diff_x * diff_x + diff_y * diff_y) * scale)


def factors(scale_ref):
    return [-0.5 / (scale_ref[i] * scale_ref[i]) for i in range(3)]


CHUNK = 1024


def pack_global(out_ref, upper):
    rows = [
        upper[:H, :H],
        upper[H:, :H],
        upper[H:, H:R],
        jnp.concatenate([upper[:H, R:], upper[H:, R:]], axis=1),
    ]
    out_ref[...] = jnp.concatenate(rows, axis=0).reshape(out_ref.shape)


def pack_regional(out_ref, m):
    q = H // 2
    out_ref[0:H, :] = m[H:, :H]
    out_ref[H : H + q, :] = m[q:H, :H]
    out_ref[H + q : 2 * H, :] = m[H + q :, H:]
    out_ref[2 * H : 2 * H + q, :] = jnp.concatenate([m[:q, :q], m[H : H + q, H : H + q]], axis=1)


def regional_of(ref):
    q = H // 2
    corners = ref[2 * H : 2 * H + q, :]
    blocks = [ref[0:H, :]]
    for n in range(2):
        low = ref[H + n * q : H + (n + 1) * q, :]
        top = jnp.concatenate([corners[:, n * q : (n + 1) * q], low[:, :q].T], axis=1)
        blocks.append(jnp.concatenate([top, low], axis=0))
    b, a, c = blocks
    return jnp.concatenate(
        [jnp.concatenate([a, b.T], axis=1), jnp.concatenate([b, c], axis=1)], axis=0
    )


def whole_of(packed):
    a, b, c = (packed[n * H : (n + 1) * H, :] for n in range(3))
    return jnp.concatenate(
        [jnp.concatenate([a, b.T], axis=1), jnp.concatenate([b, c], axis=1)], axis=0
    )


def fields_of(ref, block):
    y = ref[block * H : (block + 1) * H, :]
    return jnp.concatenate([y[:, :FIELDS], y[:, FIELDS:]], axis=0)


def shape(*dims):
    return jax.ShapeDtypeStruct(dims, F32)


NY, NX, NZ, NC = 8, 4, 8, 2
GROUP = [(dx, dc) for dx in range(NX) for dc in range(NC)][1:]
NEAREST = sorted(range(NY), key=lambda d: min(d, NY - d))
FARTHEST = NEAREST[:0:-1]
PLANE = [(dx, dy) for dy in NEAREST[::-1] for dx in range(NX) if (dx, dy) != (0, 0)]


def here():
    return (
        lax.axis_index("region"),
        lax.axis_index("super_0"),
        lax.axis_index("super_1"),
        lax.axis_index("super_2"),
    )


def on_y(d):
    y, x, z, c = here()
    return (lax.rem(y + d, NY), x, z, c)


def on_z(d):
    y, x, z, c = here()
    return (y, x, lax.rem(z + d, NZ), c)


def on_xc(d):
    y, x, z, c = here()
    return (y, lax.rem(x + d[0], NX), z, lax.rem(c + d[1], NC))


def on_xy(d):
    y, x, z, c = here()
    return (lax.rem(y + d[1], NY), lax.rem(x + d[0], NX), z, c)


def greet(places):
    barrier = pltpu.get_barrier_semaphore()
    for place in places:
        pl.semaphore_signal(barrier, inc=1, device_id=place, device_id_type=MESH)
    return lambda: pl.semaphore_wait(barrier, len(places))


def send(source, target, sems, n, place):
    copy = pltpu.make_async_remote_copy(
        src_ref=source,
        dst_ref=target,
        send_sem=sems[0].at[n],
        recv_sem=sems[1].at[n],
        device_id=place,
        device_id_type=MESH,
    )
    copy.start()
    return copy


def arrived(copies):
    for copy in copies:
        copy.wait_recv()


def sent(copies):
    for copy in copies:
        copy.wait_send()


def added(own, arrivals_ref):
    return total_of([own] + [arrivals_ref[n] for n in range(arrivals_ref.shape[0])])


def pair_of_sems(count):
    return [pltpu.SemaphoreType.DMA((count,)), pltpu.SemaphoreType.DMA((count,))]


M_ROWS, C_ROWS = 5 * H // 2, 5 * H
M_PART, C_PART = M_ROWS // NY, C_ROWS // NY
EXCHANGES = (7, 7, 7, 7, 7, 7, 7, 7, 31, 8)
CROSS_STEP = 0


def kernel(*refs):
    it = iter(refs)
    take = lambda n: [next(it) for _ in range(n)]
    (scale_ref,) = take(1)
    sources = take(10)
    (out_ref,) = take(1)
    targets = take(10)
    (copy_sems,) = take(1)
    sems = [take(2) for _ in EXCHANGES]
    z_refs = take(2)
    gv_ref, gr_ref, gg_ref, w_ref, d_ref, t2_ref, table_ref = take(7)
    mc_ref, gs_ref, m_ref, c_ref, m_in, c_in, g_in, g_sum, y_in = take(9)
    corr_ref, k_in, z_in, up_ref = take(4)
    elim = take(7)
    f_ref = elim[0]
    gk_ref, rk_ref, lk_ref, coords_ref, precision_ref, values_ref, sites_ref, prior_l, prior_r, prior_g = targets

    copies = [
        pltpu.make_async_copy(a, b, copy_sems.at[n]) for n, (a, b) in enumerate(zip(sources, targets))
    ]
    for copy in copies:
        copy.start()
    y, x, z, c = here()
    met = greet(
        [on_xy(d) for d in PLANE]
        + [on_xc(d) for d in GROUP if d[1]]
        + [on_z(d) for d in range(1, NZ)]
    )
    for copy in copies[:6]:
        copy.wait()
    started = []

    scale = factors(scale_ref)
    knots = [upright(lk_ref[...]), upright(rk_ref[...]), upright(gk_ref[...])]
    scales = [scale[2], scale[1], scale[0]]
    grams = (gv_ref, gr_ref, gg_ref)
    chunks = coords_ref.shape[1] // CHUNK

    def fill(z_ref, i):
        at = pl.ds(i * CHUNK, CHUNK)
        places = coords_ref[:, at]
        weight = jnp.sqrt(precision_ref[:, at])
        z_ref[:FIELDS, :] = (values_ref[:, at].astype(F32) * weight).astype(BF16)
        for n in range(3):
            first = FIELDS + n * R
            z_ref[first : first + R, :] = (basis(knots[n], places, scales[n]) * weight).astype(BF16)

    fill(z_refs[0], 0)
    for i in range(chunks):
        now, later = z_refs[i % 2], z_refs[(i + 1) % 2]
        if i + 1 < chunks:
            fill(later, i + 1)
        for n, ref in enumerate(grams):
            first = FIELDS + n * R
            block = gram_of(now[: first + R, :], now[first : first + R, :])
            ref[...] = block if i == 0 else ref[...] + block
    for copy in copies[6:]:
        copy.wait()
    f_ref[...] = prior_l[...] + gv_ref[FIELDS:, :]
    eliminate(*elim[:1], w_ref, d_ref, *elim[1:])

    def scatter(rows, first, part, target, pair):
        copies = []
        for d in FARTHEST:
            place = on_y(d)
            at = pl.ds(pl.multiple_of(first + place[0] * part, 8), part)
            copies.append(send(rows.at[at, :], target.at[d - 1], pair, d - 1, place))
        started.extend(copies)
        return copies

    def gather(ref, part, pair):
        at = pl.ds(pl.multiple_of(y * part, 8), part)
        copies = [send(ref.at[at, :], ref.at[at, :], pair, d - 1, on_y(d)) for d in FARTHEST]
        started.extend(copies)
        return copies

    leaf_rows = slice(FIELDS, FIELDS + R)
    region_rows = slice(FIELDS + R, FIELDS + 2 * R)
    t1 = dot(w_ref[...], gr_ref[leaf_rows, :])
    t2_ref[:, :R] = scaled(t1, d_ref)
    regional = gr_ref[region_rows, :] - dot_t(t1, t2_ref[:, :R])
    pack_regional(mc_ref, regional)
    met()
    m_scatter = scatter(mc_ref, 0, M_PART, m_in, sems[0])
    right = jnp.concatenate([gg_ref[leaf_rows, :], gv_ref[:FIELDS, :].T], axis=1)
    t1_right = dot(w_ref[...], right)
    t2_ref[:, R:] = scaled(t1_right, d_ref)
    regional = jnp.concatenate([gg_ref[region_rows, :], gr_ref[:FIELDS, :].T], axis=1) - dot_t(
        t1, t2_ref[:, R:]
    )
    for r in range(2):
        for n in range(2):
            k = M_ROWS + (2 * r + n) * H
            mc_ref[k : k + H, :] = regional[r * H : (r + 1) * H, n * H : (n + 1) * H]
    mc_ref[M_ROWS + 4 * H :, :] = jnp.concatenate([regional[:H, R:], regional[H:, R:]], axis=1)
    c_scatter = scatter(mc_ref, M_ROWS, C_PART, c_in, sems[3])
    upper = jnp.concatenate([gg_ref[FIELDS + 2 * R :, :], gg_ref[:FIELDS, :].T], axis=1)
    pack_global(gs_ref, upper - dot_t(t1_right[:, :R], t2_ref[:, R:]))
    g_scatter = []
    for n, d in enumerate(GROUP):
        place = on_xc(d)
        g_scatter.append(send(gs_ref.at[place[3], :, place[1]], g_in.at[n], sems[1], n, place))
    started.extend(g_scatter)
    arrived(m_scatter)
    own = pl.ds(pl.multiple_of(y * M_PART, 8), M_PART)
    m_ref[own, :] = added(mc_ref[own, :], m_in)
    m_gather = gather(m_ref, M_PART, sems[2])

    places = sites_ref[...]
    sites_l = dot(w_ref[...], basis(knots[0], places, scales[0]))
    seen = dot_t(t2_ref[...], sites_l)
    table_ref[:R, :] = basis(knots[1], places, scales[1]) - seen[:R]
    table_ref[R : 2 * R, :] = basis(knots[2], places, scales[2]) - seen[R : 2 * R]
    table_ref[2 * R :, :] = seen[2 * R :]

    arrived(m_gather)
    f_ref[...] = prior_r[...] + regional_of(m_ref)
    later = {}

    def send_cross():
        arrived(c_scatter)
        mine = pl.ds(pl.multiple_of(y * C_PART, 8), C_PART)
        theirs = pl.ds(pl.multiple_of(M_ROWS + y * C_PART, 8), C_PART)
        c_ref[mine, :] = added(mc_ref[theirs, :], c_in)
        later["c"] = gather(c_ref, C_PART, sems[4])

    def send_share():
        arrived(g_scatter)
        g_sum[...] = added(gs_ref[c, :, x], g_in)
        later["y"] = []
        for d in range(1, NY):
            place = on_y(d)
            later["y"].append(send(g_sum.at[place[0]], y_in.at[d - 1], sems[5], d - 1, place))
        started.extend(later["y"])

    eliminate(*elim[:1], w_ref, d_ref, *elim[1:], hooks=[(CROSS_STEP, send_cross), (20, send_share)])
    arrived(later["c"])
    cross = jnp.concatenate(
        [
            jnp.concatenate([c_ref[(2 * r + n) * H : (2 * r + n + 1) * H, :] for n in range(2)], axis=1)
            for r in range(2)
        ],
        axis=0,
    )
    t1 = dot(w_ref[...], jnp.concatenate([cross, fields_of(c_ref, 4)], axis=1))
    t2_ref[:, : R + FIELDS] = scaled(t1, d_ref)
    pack_global(corr_ref, dot_t(t1[:, :R], t2_ref[:, : R + FIELDS]))

    first = []
    for n, d in enumerate(GROUP):
        place = on_xc(d)
        first.append(send(corr_ref.at[place[3], y, place[1]], k_in.at[n], sems[6], n, place))
    arrived(later["y"])
    share = added(g_sum[y], y_in)
    arrived(first)
    z_in[z] = share - added(corr_ref[c, y, x], k_in)
    second = [send(z_in.at[z], z_in.at[z], sems[7], d - 1, on_z(d)) for d in FARTHEST]
    sites_r = dot(w_ref[...], table_ref[:R, :])
    seen = dot_t(t2_ref[:, : R + FIELDS], sites_r)
    table_ref[R : 2 * R, :] -= seen[:R]
    table_ref[2 * R :, :] += seen[R:]
    arrived(second)
    up_ref[c, y, x] = total_of([z_in[n] for n in range(NZ)])
    third = {}
    for n, d in enumerate(PLANE):
        third[d] = send(up_ref.at[c, y, x], up_ref.at[c, y, x], sems[8], n, on_xy(d))
    fourth = []
    for dy in NEAREST:
        for dx in range(NX):
            if (dx, dy) != (0, 0):
                third[dx, dy].wait_recv()
        block = up_ref.at[c, lax.rem(y - dy + NY, NY)]
        fourth.append(send(block, block, sems[9], dy, on_xc((0, 1))))
    arrived(fourth)
    upper = up_ref[...].reshape(4 * H, H)
    f_ref[...] = prior_g[...] + whole_of(upper)
    eliminate(*elim[:1], w_ref, d_ref, *elim[1:])
    nsite = table_ref.shape[1]
    t1 = dot(w_ref[...], jnp.concatenate([table_ref[R : 2 * R, :], fields_of(upper, 3)], axis=1))
    out_ref[...] = table_ref[2 * R :, :] + dot_t(scaled(t1[:, nsite:], d_ref), t1[:, :nsite])
    sent(started + first + second + list(third.values()) + fourth)


def everything(scales, *operands):
    sites = operands[6]
    sems = []
    for count in EXCHANGES:
        sems += pair_of_sems(count)
    tiles = pltpu.VMEM((NC, NY, NX, B, H), F32)
    return pl.pallas_call(
        kernel,
        name="all",
        out_shape=shape(FIELDS, sites.shape[1]),
        in_specs=[SMEM] + [pl.BlockSpec(memory_space=pl.ANY)] * len(operands),
        out_specs=VMEM,
        scratch_shapes=[pltpu.VMEM(a.shape, a.dtype) for a in operands]
        + [pltpu.SemaphoreType.DMA((len(operands),))]
        + sems
        + [
            pltpu.VMEM((3 * R + FIELDS, CHUNK), BF16),
            pltpu.VMEM((3 * R + FIELDS, CHUNK), BF16),
            pltpu.VMEM((FIELDS + R, R), F32),
            pltpu.VMEM((FIELDS + 2 * R, R), F32),
            pltpu.VMEM((FIELDS + 3 * R, R), F32),
            pltpu.VMEM((R, R), F32),
            pltpu.VMEM((R, H), F32),
            pltpu.VMEM((R, 2 * R + FIELDS), F32),
            pltpu.VMEM((2 * R + FIELDS, sites.shape[1]), F32),
            pltpu.VMEM((M_ROWS + C_ROWS, H), F32),
            tiles,
            pltpu.VMEM((M_ROWS, H), F32),
            pltpu.VMEM((C_ROWS, H), F32),
            pltpu.VMEM((NY - 1, M_PART, H), F32),
            pltpu.VMEM((NY - 1, C_PART, H), F32),
            pltpu.VMEM((7, NY, B, H), F32),
            pltpu.VMEM((NY, B, H), F32),
            pltpu.VMEM((NY - 1, B, H), F32),
            tiles,
            pltpu.VMEM((7, B, H), F32),
            pltpu.VMEM((NZ, B, H), F32),
            tiles,
        ]
        + eliminate_scratch(),
        compiler_params=pltpu.CompilerParams(
            vmem_limit_bytes=LIMIT, collective_id=0, has_side_effects=True
        ),
    )(scales, *operands)


def shards(
    obs_coords,
    obs_values,
    obs_precision,
    site_coords,
    length_scale,
    global_knots,
    region_knots,
    leaf_knots,
    global_prior,
    region_prior,
    leaf_prior,
):
    return everything(
        length_scale,
        global_knots,
        region_knots[0],
        leaf_knots[0],
        obs_coords,
        obs_precision[None],
        obs_values,
        site_coords,
        leaf_prior[0],
        region_prior[0],
        global_prior,
    )


def solution(mesh):
    split = Mesh(
        mesh.devices.reshape(NY, NX, NZ, NC),
        ("region", "super_0", "super_1", "super_2"),
    )
    return jax.shard_map(
        shards,
        mesh=split,
        in_specs=(
            P(None, REGION_SUPER),
            P(None, REGION_SUPER),
            P(REGION_SUPER),
            P(None, REGION_SUPER),
            P(),
            P(),
            P(SUPER, None, None),
            P(REGION_SUPER, None, None),
            P(),
            P(SUPER, None, None),
            P(REGION_SUPER, None, None),
        ),
        out_specs=P(None, REGION_SUPER),
        check_vma=False,
    )
```

```python
import functools

import jax
import jax.numpy as jnp
from jax import lax
from jax.experimental import pallas as pl
from jax.experimental.pallas import tpu as pltpu
from jax.sharding import Mesh
from jax.sharding import PartitionSpec as P

R = 256
B = 8
H = 128
FIELDS = 64
F32 = jnp.float32
BF16 = jnp.bfloat16
HIGH = lax.Precision.HIGHEST
MESH = pl.DeviceIdType.MESH
REGION_SUPER = ("region", "super_0", "super_1", "super_2")
SUPER = ("super_0", "super_1", "super_2")
VMEM = pl.BlockSpec(memory_space=pltpu.VMEM)
SMEM = pl.BlockSpec(memory_space=pltpu.SMEM)
LIMIT = 60 * 1024 * 1024


def parts_of(x):
    high = x.astype(BF16).astype(F32)
    rest = x - high
    middle = rest.astype(BF16).astype(F32)
    return high, middle, rest - middle


def left_stack(x):
    h, m, l = parts_of(x)
    return jnp.concatenate([h, h, m, h, l, m], axis=0).astype(BF16)


def right_stack(x):
    h, m, l = parts_of(x)
    return jnp.concatenate([h, m, h, l, h, m], axis=0).astype(BF16)


def total_of(terms):
    terms = list(terms)
    while len(terms) > 1:
        pairs = [terms[i] + terms[i + 1] for i in range(0, len(terms) - 1, 2)]
        terms = pairs + terms[len(pairs) * 2 :]
    return terms[0]


def columns_of(x, first):
    zero = jnp.zeros((B, H), jnp.int32)
    return [jnp.take_along_axis(x, zero + (first + j), axis=1) for j in range(B)]


def row_of(ref, r):
    return jnp.broadcast_to(ref[r : r + 1, :], (B, ref.shape[1]))


def twice(x):
    return jnp.concatenate([x, x], axis=1)


def eliminate(f_ref, w_ref, d_ref, cols_ref, rows_ref, mine_ref, x_ref, lh_ref, xh_ref, hooks=()):
    lane = lax.broadcasted_iota(jnp.int32, (B, R), 1)
    sub = lax.broadcasted_iota(jnp.int32, (B, R), 0)
    sub_half = lax.broadcasted_iota(jnp.int32, (B, H), 0)
    for ref in (mine_ref, x_ref, lh_ref, xh_ref):
        ref[...] = jnp.zeros_like(ref)

    def body(first, k, panel):
        base = pl.multiple_of(k * B, B)
        half = lax.div(k, 16)
        at = (k - 16 * half) * B
        diag = jnp.where(half == 0, panel[:, :H], panel[:, H:])
        for j, column in enumerate(columns_of(diag, at)):
            cols_ref[j * B : (j + 1) * B, :] = column
        mark = (lane >= base) & (lane < base + B)
        eye = jnp.where(lane == base + sub, 1.0, 0.0).astype(F32)
        rows_ref[...] = jnp.where(mark, eye, panel)
        following = pl.multiple_of(jnp.minimum(k + 1, R // B - 1) * B, B)
        ahead = f_ref[pl.ds(following, B), :]
        next_half = lax.div(following, H)
        next_at = following - next_half * H + sub_half

        def upright_of(row):
            part = jnp.where(next_half == 0, row[:, :H], row[:, H:])
            return jnp.take_along_axis(part, next_at, axis=1)

        keep = jnp.where((lane >= base - B) & (lane < base), 0.0, 1.0).astype(F32)
        before = [upright_of(row_of(mine_ref, j)) for j in range(B)]
        ahead = ahead * keep - total_of([twice(before[j]) * row_of(x_ref, j) for j in range(B)])
        f_ref[first:, :] = f_ref[first:, :] * keep[0:1, :] - lax.dot_general(
            lh_ref[:, first:], xh_ref[...], (((0,), (0,)), ((), ())), preferred_element_type=F32
        )
        rows = [row_of(rows_ref, j) for j in range(B)]
        g = [upright_of(row) for row in rows]
        s = {}
        for j in range(B):
            for i in range(j + 1):
                s[i, j] = row_of(cols_ref, j * B + i)
        low = {}
        inv = []
        for p in range(B):
            inv.append(1.0 / s[p, p])
            for i in range(p + 1, B):
                m = s[p, i] * inv[p]
                for j in range(i, B):
                    s[i, j] = s[i, j] - m * s[p, j]
                for c in range(p):
                    low[i, c] = low[i, c] - m * low[p, c]
                low[i, p] = -m
        row = [total_of([twice(low[j, m]) * rows[m] for m in range(j)] + [rows[j]]) for j in range(B)]
        lcol = [total_of([g[m] * low[j, m] for m in range(j)] + [g[j]]) * inv[j] for j in range(B)]
        panel_next = jnp.where(mark, 0.0, ahead) - total_of([twice(lcol[j]) * row[j] for j in range(B)])
        dcol = inv[0]
        mine = row[0]
        for i in range(1, B):
            dcol = jnp.where(sub_half == i, inv[i], dcol)
            mine = jnp.where(sub == i, row[i], mine)
        x = twice(dcol) * mine
        done = lane < base + B
        w_ref[pl.ds(base, B), :] = jnp.where(done, mine, 0.0)
        d_ref[pl.ds(base, B), :] = dcol
        mine_ref[...] = mine
        x_ref[...] = x
        lh_ref[...] = left_stack(jnp.where(done, 0.0, mine))
        xh_ref[...] = right_stack(x)
        return panel_next

    panel = f_ref[0:B, :]
    at = 0
    for stop, hook in sorted([*hooks, (R // B // 2, None), (R // B, None)], key=lambda h: h[0]):
        if stop > at:
            first = H if at >= R // B // 2 else 0
            panel = lax.fori_loop(at, stop, functools.partial(body, first), panel)
            at = stop
        if hook is not None:
            hook()


def eliminate_scratch():
    return [
        pltpu.VMEM((R, R), F32),
        pltpu.VMEM((B * B, H), F32),
        pltpu.VMEM((B, R), F32),
        pltpu.VMEM((B, R), F32),
        pltpu.VMEM((B, R), F32),
        pltpu.VMEM((48, R), BF16),
        pltpu.VMEM((48, R), BF16),
    ]


def dot(a, b):
    return jnp.dot(a, b, precision=HIGH, preferred_element_type=F32)


def dot_t(a, b):
    return lax.dot_general(a, b, (((0,), (0,)), ((), ())), precision=HIGH, preferred_element_type=F32)


def scaled(t, d_ref):
    whole, rest = divmod(t.shape[1], H)
    d = d_ref[...]
    return t * jnp.concatenate([d] * whole + [d[:, :rest]] * (rest > 0), axis=1)


def gram_of(a, b):
    return lax.dot_general(a, b, (((1,), (1,)), ((), ())), preferred_element_type=F32)


def upright(knots):
    spare = jnp.zeros((6, R), F32)
    return jnp.concatenate([knots, spare], axis=0).T


def basis(knots, places, scale):
    diff_x = knots[:, 0:1] - places[0:1, :]
    diff_y = knots[:, 1:2] - places[1:2, :]
    return jnp.exp((diff_x * diff_x + diff_y * diff_y) * scale)


def factors(scale_ref):
    return [-0.5 / (scale_ref[i] * scale_ref[i]) for i in range(3)]


CHUNK = 1024


def pack_global(out_ref, upper):
    rows = [
        upper[:H, :H],
        upper[H:, :H],
        upper[H:, H:R],
        jnp.concatenate([upper[:H, R:], upper[H:, R:]], axis=1),
    ]
    out_ref[...] = jnp.concatenate(rows, axis=0).reshape(out_ref.shape)


def pack_regional(out_ref, m):
    q = H // 2
    out_ref[0:H, :] = m[H:, :H]
    out_ref[H : H + q, :] = m[q:H, :H]
    out_ref[H + q : 2 * H, :] = m[H + q :, H:]
    out_ref[2 * H : 2 * H + q, :] = jnp.concatenate([m[:q, :q], m[H : H + q, H : H + q]], axis=1)


def regional_of(ref):
    q = H // 2
    corners = ref[2 * H : 2 * H + q, :]
    blocks = [ref[0:H, :]]
    for n in range(2):
        low = ref[H + n * q : H + (n + 1) * q, :]
        top = jnp.concatenate([corners[:, n * q : (n + 1) * q], low[:, :q].T], axis=1)
        blocks.append(jnp.concatenate([top, low], axis=0))
    b, a, c = blocks
    return jnp.concatenate(
        [jnp.concatenate([a, b.T], axis=1), jnp.concatenate([b, c], axis=1)], axis=0
    )


def whole_of(packed):
    a, b, c = (packed[n * H : (n + 1) * H, :] for n in range(3))
    return jnp.concatenate(
        [jnp.concatenate([a, b.T], axis=1), jnp.concatenate([b, c], axis=1)], axis=0
    )


def fields_of(ref, block):
    y = ref[block * H : (block + 1) * H, :]
    return jnp.concatenate([y[:, :FIELDS], y[:, FIELDS:]], axis=0)


def shape(*dims):
    return jax.ShapeDtypeStruct(dims, F32)


NY, NX, NZ, NC = 8, 4, 8, 2
GROUP = [(dx, dc) for dx in range(NX) for dc in range(NC)][1:]
NEAREST = sorted(range(NY), key=lambda d: min(d, NY - d))
FARTHEST = NEAREST[:0:-1]
PLANE = [(dx, dy) for dy in NEAREST[::-1] for dx in range(NX) if (dx, dy) != (0, 0)]


def here():
    return (
        lax.axis_index("region"),
        lax.axis_index("super_0"),
        lax.axis_index("super_1"),
        lax.axis_index("super_2"),
    )


def on_y(d):
    y, x, z, c = here()
    return (lax.rem(y + d, NY), x, z, c)


def on_z(d):
    y, x, z, c = here()
    return (y, x, lax.rem(z + d, NZ), c)


def on_xc(d):
    y, x, z, c = here()
    return (y, lax.rem(x + d[0], NX), z, lax.rem(c + d[1], NC))


def on_xy(d):
    y, x, z, c = here()
    return (lax.rem(y + d[1], NY), lax.rem(x + d[0], NX), z, c)


def greet(places):
    barrier = pltpu.get_barrier_semaphore()
    for place in places:
        pl.semaphore_signal(barrier, inc=1, device_id=place, device_id_type=MESH)
    return lambda: pl.semaphore_wait(barrier, len(places))


def send(source, target, sems, n, place):
    copy = pltpu.make_async_remote_copy(
        src_ref=source,
        dst_ref=target,
        send_sem=sems[0].at[n],
        recv_sem=sems[1].at[n],
        device_id=place,
        device_id_type=MESH,
    )
    copy.start()
    return copy


def arrived(copies):
    for copy in copies:
        copy.wait_recv()


def sent(copies):
    for copy in copies:
        copy.wait_send()


def added(own, arrivals_ref):
    return total_of([own] + [arrivals_ref[n] for n in range(arrivals_ref.shape[0])])


def pair_of_sems(count):
    return [pltpu.SemaphoreType.DMA((count,)), pltpu.SemaphoreType.DMA((count,))]


M_ROWS, C_ROWS = 5 * H // 2, 5 * H
M_PART, C_PART = M_ROWS // NY, C_ROWS // NY
EXCHANGES = (7, 7, 7, 7, 7, 7, 7, 7, 31, 8)


def kernel(*refs):
    it = iter(refs)
    take = lambda n: [next(it) for _ in range(n)]
    (scale_ref,) = take(1)
    sources = take(10)
    (out_ref,) = take(1)
    targets = take(10)
    (copy_sems,) = take(1)
    sems = [take(2) for _ in EXCHANGES]
    z_refs = take(2)
    gv_ref, gr_ref, gg_ref, w_ref, d_ref, t2_ref, table_ref = take(7)
    mc_ref, gs_ref, m_ref, c_ref, m_in, c_in, g_in, g_sum, y_in = take(9)
    corr_ref, k_in, z_in, up_ref = take(4)
    elim = take(7)
    f_ref = elim[0]
    gk_ref, rk_ref, lk_ref, coords_ref, precision_ref, values_ref, sites_ref, prior_l, prior_r, prior_g = targets

    copies = [
        pltpu.make_async_copy(a, b, copy_sems.at[n]) for n, (a, b) in enumerate(zip(sources, targets))
    ]
    for copy in copies:
        copy.start()
    y, x, z, c = here()
    met = greet(
        [on_xy(d) for d in PLANE]
        + [on_xc(d) for d in GROUP if d[1]]
        + [on_z(d) for d in range(1, NZ)]
    )
    for copy in copies[:6]:
        copy.wait()
    started = []

    scale = factors(scale_ref)
    knots = [upright(lk_ref[...]), upright(rk_ref[...]), upright(gk_ref[...])]
    scales = [scale[2], scale[1], scale[0]]
    grams = (gv_ref, gr_ref, gg_ref)
    chunks = coords_ref.shape[1] // CHUNK

    def fill(z_ref, i):
        at = pl.ds(i * CHUNK, CHUNK)
        places = coords_ref[:, at]
        weight = jnp.sqrt(precision_ref[:, at])
        z_ref[:FIELDS, :] = (values_ref[:, at].astype(F32) * weight).astype(BF16)
        for n in range(3):
            first = FIELDS + n * R
            z_ref[first : first + R, :] = (basis(knots[n], places, scales[n]) * weight).astype(BF16)

    fill(z_refs[0], 0)
    for i in range(chunks):
        now, later = z_refs[i % 2], z_refs[(i + 1) % 2]
        if i + 1 < chunks:
            fill(later, i + 1)
        for n, ref in enumerate(grams):
            first = FIELDS + n * R
            block = gram_of(now[: first + R, :], now[first : first + R, :])
            ref[...] = block if i == 0 else ref[...] + block
    for copy in copies[6:]:
        copy.wait()
    f_ref[...] = prior_l[...] + gv_ref[FIELDS:, :]
    eliminate(*elim[:1], w_ref, d_ref, *elim[1:])

    def scatter(rows, first, part, target, pair):
        copies = []
        for d in FARTHEST:
            place = on_y(d)
            at = pl.ds(pl.multiple_of(first + place[0] * part, 8), part)
            copies.append(send(rows.at[at, :], target.at[d - 1], pair, d - 1, place))
        started.extend(copies)
        return copies

    def gather(ref, part, pair):
        at = pl.ds(pl.multiple_of(y * part, 8), part)
        copies = [send(ref.at[at, :], ref.at[at, :], pair, d - 1, on_y(d)) for d in FARTHEST]
        started.extend(copies)
        return copies

    leaf_rows = slice(FIELDS, FIELDS + R)
    region_rows = slice(FIELDS + R, FIELDS + 2 * R)
    t1 = dot(w_ref[...], gr_ref[leaf_rows, :])
    t2_ref[:, :R] = scaled(t1, d_ref)
    regional = gr_ref[region_rows, :] - dot_t(t1, t2_ref[:, :R])
    pack_regional(mc_ref, regional)
    met()
    m_scatter = scatter(mc_ref, 0, M_PART, m_in, sems[0])
    right = jnp.concatenate([gg_ref[leaf_rows, :], gv_ref[:FIELDS, :].T], axis=1)
    t1_right = dot(w_ref[...], right)
    t2_ref[:, R:] = scaled(t1_right, d_ref)
    regional = jnp.concatenate([gg_ref[region_rows, :], gr_ref[:FIELDS, :].T], axis=1) - dot_t(
        t1, t2_ref[:, R:]
    )
    for r in range(2):
        for n in range(2):
            k = M_ROWS + (2 * r + n) * H
            mc_ref[k : k + H, :] = regional[r * H : (r + 1) * H, n * H : (n + 1) * H]
    mc_ref[M_ROWS + 4 * H :, :] = jnp.concatenate([regional[:H, R:], regional[H:, R:]], axis=1)
    c_scatter = scatter(mc_ref, M_ROWS, C_PART, c_in, sems[3])
    upper = jnp.concatenate([gg_ref[FIELDS + 2 * R :, :], gg_ref[:FIELDS, :].T], axis=1)
    pack_global(gs_ref, upper - dot_t(t1_right[:, :R], t2_ref[:, R:]))
    g_scatter = []
    for n, d in enumerate(GROUP):
        place = on_xc(d)
        g_scatter.append(send(gs_ref.at[place[3], :, place[1]], g_in.at[n], sems[1], n, place))
    started.extend(g_scatter)
    arrived(m_scatter)
    own = pl.ds(pl.multiple_of(y * M_PART, 8), M_PART)
    m_ref[own, :] = added(mc_ref[own, :], m_in)
    m_gather = gather(m_ref, M_PART, sems[2])

    places = sites_ref[...]
    sites_l = dot(w_ref[...], basis(knots[0], places, scales[0]))
    seen = dot_t(t2_ref[...], sites_l)
    table_ref[:R, :] = basis(knots[1], places, scales[1]) - seen[:R]
    table_ref[R : 2 * R, :] = basis(knots[2], places, scales[2]) - seen[R : 2 * R]
    table_ref[2 * R :, :] = seen[2 * R :]

    later = {}

    def send_cross():
        arrived(c_scatter)
        mine = pl.ds(pl.multiple_of(y * C_PART, 8), C_PART)
        theirs = pl.ds(pl.multiple_of(M_ROWS + y * C_PART, 8), C_PART)
        c_ref[mine, :] = added(mc_ref[theirs, :], c_in)
        later["c"] = gather(c_ref, C_PART, sems[4])

    def send_share():
        arrived(g_scatter)
        g_sum[...] = added(gs_ref[c, :, x], g_in)
        later["y"] = []
        for d in range(1, NY):
            place = on_y(d)
            later["y"].append(send(g_sum.at[place[0]], y_in.at[d - 1], sems[5], d - 1, place))
        started.extend(later["y"])

    send_cross()
    arrived(m_gather)
    f_ref[...] = prior_r[...] + regional_of(m_ref)
    eliminate(*elim[:1], w_ref, d_ref, *elim[1:], hooks=[(20, send_share)])
    arrived(later["c"])
    cross = jnp.concatenate(
        [
            jnp.concatenate([c_ref[(2 * r + n) * H : (2 * r + n + 1) * H, :] for n in range(2)], axis=1)
            for r in range(2)
        ],
        axis=0,
    )
    t1 = dot(w_ref[...], jnp.concatenate([cross, fields_of(c_ref, 4)], axis=1))
    t2_ref[:, : R + FIELDS] = scaled(t1, d_ref)
    pack_global(corr_ref, dot_t(t1[:, :R], t2_ref[:, : R + FIELDS]))

    first = []
    for n, d in enumerate(GROUP):
        place = on_xc(d)
        first.append(send(corr_ref.at[place[3], y, place[1]], k_in.at[n], sems[6], n, place))
    arrived(later["y"])
    share = added(g_sum[y], y_in)
    arrived(first)
    z_in[z] = share - added(corr_ref[c, y, x], k_in)
    second = [send(z_in.at[z], z_in.at[z], sems[7], d - 1, on_z(d)) for d in FARTHEST]
    sites_r = dot(w_ref[...], table_ref[:R, :])
    seen = dot_t(t2_ref[:, : R + FIELDS], sites_r)
    table_ref[R : 2 * R, :] -= seen[:R]
    table_ref[2 * R :, :] += seen[R:]
    arrived(second)
    up_ref[c, y, x] = total_of([z_in[n] for n in range(NZ)])
    third = {}
    for n, d in enumerate(PLANE):
        third[d] = send(up_ref.at[c, y, x], up_ref.at[c, y, x], sems[8], n, on_xy(d))
    fourth = []
    for dy in NEAREST:
        for dx in range(NX):
            if (dx, dy) != (0, 0):
                third[dx, dy].wait_recv()
        block = up_ref.at[c, lax.rem(y - dy + NY, NY)]
        fourth.append(send(block, block, sems[9], dy, on_xc((0, 1))))
    arrived(fourth)
    upper = up_ref[...].reshape(4 * H, H)
    f_ref[...] = prior_g[...] + whole_of(upper)
    eliminate(*elim[:1], w_ref, d_ref, *elim[1:])
    nsite = table_ref.shape[1]
    t1 = dot(w_ref[...], jnp.concatenate([table_ref[R : 2 * R, :], fields_of(upper, 3)], axis=1))
    out_ref[...] = table_ref[2 * R :, :] + dot_t(scaled(t1[:, nsite:], d_ref), t1[:, :nsite])
    sent(started + first + second + list(third.values()) + fourth)


def everything(scales, *operands):
    sites = operands[6]
    sems = []
    for count in EXCHANGES:
        sems += pair_of_sems(count)
    tiles = pltpu.VMEM((NC, NY, NX, B, H), F32)
    return pl.pallas_call(
        kernel,
        name="all",
        out_shape=shape(FIELDS, sites.shape[1]),
        in_specs=[SMEM] + [pl.BlockSpec(memory_space=pl.ANY)] * len(operands),
        out_specs=VMEM,
        scratch_shapes=[pltpu.VMEM(a.shape, a.dtype) for a in operands]
        + [pltpu.SemaphoreType.DMA((len(operands),))]
        + sems
        + [
            pltpu.VMEM((3 * R + FIELDS, CHUNK), BF16),
            pltpu.VMEM((3 * R + FIELDS, CHUNK), BF16),
            pltpu.VMEM((FIELDS + R, R), F32),
            pltpu.VMEM((FIELDS + 2 * R, R), F32),
            pltpu.VMEM((FIELDS + 3 * R, R), F32),
            pltpu.VMEM((R, R), F32),
            pltpu.VMEM((R, H), F32),
            pltpu.VMEM((R, 2 * R + FIELDS), F32),
            pltpu.VMEM((2 * R + FIELDS, sites.shape[1]), F32),
            pltpu.VMEM((M_ROWS + C_ROWS, H), F32),
            tiles,
            pltpu.VMEM((M_ROWS, H), F32),
            pltpu.VMEM((C_ROWS, H), F32),
            pltpu.VMEM((NY - 1, M_PART, H), F32),
            pltpu.VMEM((NY - 1, C_PART, H), F32),
            pltpu.VMEM((7, NY, B, H), F32),
            pltpu.VMEM((NY, B, H), F32),
            pltpu.VMEM((NY - 1, B, H), F32),
            tiles,
            pltpu.VMEM((7, B, H), F32),
            pltpu.VMEM((NZ, B, H), F32),
            tiles,
        ]
        + eliminate_scratch(),
        compiler_params=pltpu.CompilerParams(
            vmem_limit_bytes=LIMIT, collective_id=0, has_side_effects=True
        ),
    )(scales, *operands)


def shards(
    obs_coords,
    obs_values,
    obs_precision,
    site_coords,
    length_scale,
    global_knots,
    region_knots,
    leaf_knots,
    global_prior,
    region_prior,
    leaf_prior,
):
    return everything(
        length_scale,
        global_knots,
        region_knots[0],
        leaf_knots[0],
        obs_coords,
        obs_precision[None],
        obs_values,
        site_coords,
        leaf_prior[0],
        region_prior[0],
        global_prior,
    )


def solution(mesh):
    split = Mesh(
        mesh.devices.reshape(NY, NX, NZ, NC),
        ("region", "super_0", "super_1", "super_2"),
    )
    return jax.shard_map(
        shards,
        mesh=split,
        in_specs=(
            P(None, REGION_SUPER),
            P(None, REGION_SUPER),
            P(REGION_SUPER),
            P(None, REGION_SUPER),
            P(),
            P(),
            P(SUPER, None, None),
            P(REGION_SUPER, None, None),
            P(),
            P(SUPER, None, None),
            P(REGION_SUPER, None, None),
        ),
        out_specs=P(None, REGION_SUPER),
        check_vma=False,
    )
```
